32 devices in a mesh: row: 4 (over x, core), col: 8 (over z, y).
Axes of the slice: x: 2, y: 2, z: 4, core: 2. Of those that a mesh axis runs over, the one named last changes fastest.
Arguments:
- filtered: float32 [8192, 2048], P(('row', 'col')), as said below
- hamiltonian_applied: float32 [8192, 2048], P(('row', 'col')), as said below
- rotation: float32 [2048, 2048], replicated, may hold values from -0.125 to 0.125
Outputs:
- intersection: float32 [2048, 2048], P('row', 'col')
- projected: float32 [2048, 2048], P('row', 'col')
- rotated: float32 [8192, 2048], P(('row', 'col'))
The draws below stay inside these ranges and needn't reach their ends.
Inputs may be any that keep to these rules, and one draw needn't show every extreme that they name: `filtered`: finite real values. `hamiltonian_applied`: finite real values.
All inputs are finite; a program needn't handle non-finite values.
Results may differ from the reference program's by a relative error of at most 0.00005.
Values sent between devices are 32-bit elements; how exact they have to be, the bound alone decides.
No kernel may reach another device: no remote copies, remote signals or barrier semaphores. Data moves between devices by JAX's collectives and lax.ppermute only.
A program may use at most 192 MiB of HBM per device.

```python
import math
import jax
import jax.numpy as jnp
from jax import lax

M = 2048
GRID = 8192


def orbital_parts(key):
    subkeys = jax.random.split(key, 6)
    row_scale = jnp.exp(jax.random.uniform(subkeys[0], (GRID, 1), jnp.float32, 0.0, math.log(10.0)))
    column_scale = jnp.exp(jax.random.uniform(subkeys[1], (1, M), jnp.float32, math.log(0.4), math.log(4.0)))
    noise = jax.random.normal(subkeys[2], (GRID, M), jnp.float32)
    orbitals = noise * row_scale * column_scale / math.sqrt(21.5)
    energy = jax.random.uniform(subkeys[4], (1, M), jnp.float32, -2.0, 2.0)
    extra = jax.random.normal(subkeys[5], (GRID, M), jnp.float32) * row_scale / math.sqrt(21.5)
    images = energy * orbitals + 0.5 * extra
    return (orbitals, images)


def draw_filtered(key, part):
    return orbital_parts(jax.random.fold_in(key, 11))[0]


def draw_hamiltonian_applied(key, part):
    return orbital_parts(jax.random.fold_in(key, 11))[1]


def bell_draw(key, shape, scale, bound, kind=jnp.bfloat16):
    array = scale * jax.random.normal(key, shape, jnp.float32)
    return jnp.clip(array, min=-bound, max=bound).astype(kind)


def setup_inputs(seed: int = 0) -> dict:
    key_list = jax.random.split(jax.random.key(seed), 4)
    filtered = draw_filtered(jax.random.fold_in(key_list[3], 71), 0)
    hamiltonian_applied = draw_hamiltonian_applied(jax.random.fold_in(key_list[3], 71), 0)
    rotation = bell_draw(key_list[2], (M, M), M ** -0.5, 0.125, jnp.float32)
    return {"filtered": filtered, "hamiltonian_applied": hamiltonian_applied, "rotation": rotation}


def reference(filtered, hamiltonian_applied, rotation):
    scale = 1.0 / GRID
    intersection = jnp.einsum("gi,gj->ij", filtered, filtered, precision=lax.Precision.HIGHEST, preferred_element_type=jnp.float32) * scale
    projected = jnp.einsum("gi,gj->ij", filtered, hamiltonian_applied, precision=lax.Precision.HIGHEST, preferred_element_type=jnp.float32) * scale
    rotated = jnp.dot(filtered, rotation, precision=lax.Precision.HIGHEST, preferred_element_type=jnp.float32)
    return intersection, projected, rotated
```

```python
import jax
import jax.numpy as jnp
from jax import lax
from jax.sharding import PartitionSpec as P


def bit_reversed(count):
    bits = count.bit_length() - 1
    return [int(format(i, f"0{bits}b")[::-1], 2) if bits else 0 for i in range(count)]


def contract(first, second):
    return lax.dot_general(
        first,
        second,
        (((0,), (0,)), ((), ())),
        precision=lax.Precision.HIGH,
        preferred_element_type=jnp.float32,
    )


def swap(value, axis, bit):
    count = lax.axis_size(axis)
    return lax.ppermute(value, axis, [(i, i ^ (1 << bit)) for i in range(count)])


def halve(part, dim, axis, bit):
    mine = (lax.axis_index(axis) >> bit) & 1
    half = part.shape[dim] // 2
    keep = lax.dynamic_slice_in_dim(part, mine * half, half, dim)
    send = lax.dynamic_slice_in_dim(part, (1 - mine) * half, half, dim)
    return keep + swap(send, axis, bit)


def scatter_sum(part):
    rows, cols = lax.axis_size("row"), lax.axis_size("col")
    for bit in range(rows.bit_length() - 1):
        part = halve(part, 0, "row", bit)
    for bit in range(1, cols.bit_length() - 1):
        part = halve(part, 1, "col", bit)
    return part


def local(filtered, hamiltonian_applied, rotation):
    cells, orbitals = filtered.shape
    R, C = lax.axis_size("row"), lax.axis_size("col")
    Z = C // 2
    b = orbitals // C
    scale = 1.0 / (cells * C * R)
    r, c = lax.axis_index("row"), lax.axis_index("col")
    z, y = c // 2, c % 2
    row_order, col_order = bit_reversed(R), bit_reversed(Z)

    def pick(array, parity):
        return lax.dynamic_index_in_dim(array.reshape(cells, -1, 2, b), parity, 2, keepdims=False)

    psi_own, psi_other = pick(filtered, y), pick(filtered, 1 - y)
    ham_own, ham_other = pick(hamiltonian_applied, y), pick(hamiltonian_applied, 1 - y)
    near = jnp.concatenate([psi_own, swap(psi_other, "col", 0)], 0)
    ham = jnp.concatenate([ham_own, swap(ham_other, "col", 0)], 0)
    far = jnp.concatenate([psi_other, swap(psi_own, "col", 0)], 0)

    def side(blocks, order):
        return jnp.concatenate([blocks[:, i] for i in order], 1)

    ham_cols = side(ham, col_order)
    proj_near = scatter_sum(contract(side(near, row_order), ham_cols))

    over = jnp.concatenate(
        [
            contract(
                jnp.concatenate([near[:, i] if i <= j else far[:, i] for i in row_order], 1),
                near[:, j],
            )
            for j in col_order
        ],
        1,
    )
    half = b // 2
    piece = half // Z
    odd = jnp.where(y == 0, far[:, :, :half], near[:, :, half:])
    even = jnp.where(y == 0, near, far)
    parts = []
    for n, i in enumerate(row_order):
        extra = contract(odd[:, i], even[:, i])
        extra = jnp.concatenate([extra[j * piece : (j + 1) * piece] for j in col_order], 1)
        parts += [over[n * b : (n + 1) * b], extra]
    over = scatter_sum(jnp.concatenate(parts, 0)) * scale
    main, extra = over[:b], over[b:]
    later = (r > z).astype(jnp.int32)
    h = y ^ later
    pairs = [
        (i * C + 2 * j + p, j * C + 2 * i + (p ^ int(i > j)))
        for i in range(R)
        for j in range(Z)
        for p in range(2)
        if i != j
    ]
    mirrored = lax.ppermute(main.T, ("row", "col"), pairs)
    whole = lax.all_gather(extra, "col", axis=0)
    whole = whole.reshape(Z, 2, piece, b).transpose(1, 0, 2, 3).reshape(b, b)
    mirrored = jnp.where(r == z, jnp.where(y == 0, whole, whole.T), mirrored)
    intersection = jnp.where(
        h == 0, jnp.concatenate([main, mirrored], 0), jnp.concatenate([mirrored, main], 0)
    )

    proj_far = scatter_sum(contract(side(far, row_order), ham_cols))
    projected = scale * jnp.where(
        y == 0,
        jnp.concatenate([proj_near, proj_far], 0),
        jnp.concatenate([proj_far, proj_near], 0),
    )
    rotated = jnp.dot(
        filtered, rotation, precision=lax.Precision.HIGH, preferred_element_type=jnp.float32
    )
    return (intersection, projected, rotated)


def solution(mesh):
    return jax.shard_map(
        local,
        mesh=mesh,
        in_specs=(P(("row", "col"), None), P(("row", "col"), None), P()),
        out_specs=(P("row", "col"), P("row", "col"), P(("row", "col"), None)),
        check_vma=False,
    )
```

```python
import jax
import jax.numpy as jnp
from jax import lax
from jax.experimental import pallas as pl
from jax.experimental.pallas import tpu as pltpu
from jax.sharding import PartitionSpec as P


VMEM_LIMIT = 48 * 2**20


def split(value):
    high = value.astype(jnp.bfloat16)
    return high, (value - high.astype(jnp.float32)).astype(jnp.bfloat16)


def multiply(left, right):
    dot = lambda a, b: jnp.dot(a, b, preferred_element_type=jnp.float32)
    (lh, ll), (rh, rl) = left, right
    return dot(lh, rh) + (dot(ll, rh) + dot(lh, rl))


class Device:
    def __init__(self, orbitals):
        self.R, self.C = lax.axis_size("row"), lax.axis_size("col")
        self.X, self.Z = self.R // 2, self.C // 2
        self.b = orbitals // self.C
        r, c = lax.axis_index("row"), lax.axis_index("col")
        self.r, self.c, self.y, self.z = r, c, c % 2, c // 2
        x_bits = self.X.bit_length() - 1
        z_bits = self.Z.bit_length() - 1
        self.bits = [r % 2, self.y]
        self.bits += [(r >> (1 + i)) & 1 for i in range(x_bits)]
        self.bits += [(self.z >> i) & 1 for i in range(z_bits)]
        self.x_top = 1 + x_bits
        self.x_rest = list(range(2, 1 + x_bits))
        self.z_bits = list(range(2 + x_bits, 2 + x_bits + z_bits))
        self.at = jnp.stack(self.bits + [r, self.z]).astype(jnp.int32)
        self.last, self.waits = None, []

    def axis_bit(self, bit):
        if bit < self.z_bits[0]:
            return "row", bit - 1
        return "col", bit - self.z_bits[0] + 1

    def swap(self, value, bit):
        axis, shift = self.axis_bit(bit)
        return flip(value, axis, 1 << shift)

    def wait(self, total):
        self.waits += total.terms[-1][0]

    def call(self, body, name, arrays, in_specs, out_shapes, out_specs, grid=(), scratch=()):
        after = ([] if self.last is None else [self.last]) + self.waits
        self.waits = []
        count = len(arrays)

        def ordered(at, *refs):
            body(at, *refs[:count], *refs[count + len(after) :])

        outs = pl.pallas_call(
            ordered,
            name=name,
            out_shape=[jax.ShapeDtypeStruct(s, jnp.float32) for s in out_shapes],
            grid_spec=pltpu.PrefetchScalarGridSpec(
                num_scalar_prefetch=1,
                grid=grid,
                in_specs=list(in_specs) + [pl.BlockSpec(memory_space=pl.ANY)] * len(after),
                out_specs=list(out_specs),
                scratch_shapes=list(scratch),
            ),
            compiler_params=pltpu.CompilerParams(vmem_limit_bytes=VMEM_LIMIT),
            cost_estimate=pl.CostEstimate(flops=0, bytes_accessed=0, transcendentals=0),
        )(self.at, *arrays, *after)
        self.last = outs[0]
        return outs


def flip(value, axis, mask):
    count = lax.axis_size(axis)
    return lax.ppermute(value, axis, [(i, i ^ mask) for i in range(count)])


VMEM = pl.BlockSpec(memory_space=pltpu.VMEM)


def after(value, other):
    return lax.optimization_barrier((value, other))[0]


def whole(array):
    return pl.BlockSpec(array.shape, lambda i, at: (0,) * array.ndim)


def part(dev, name, array):
    cells, b = array.shape[0], dev.b

    def body(at, source, own, other):
        even, odd = source[:, :b], source[:, b:]
        first = at[1] == 0
        own[...] = jnp.where(first, even, odd)
        other[...] = jnp.where(first, odd, even)

    block = lambda width: pl.BlockSpec((cells, width), lambda i, at: (0, i))
    return dev.call(
        body, name, [array], [block(2 * b)], [(cells, dev.R * b)] * 2,
        [block(b)] * 2, grid=(dev.R,),
    )


def part_cores(dev, own, other, image):
    cells, b, X, Z = own.shape[0], dev.b, dev.X, dev.Z
    n = Z * b

    def body(at, image, other, own, for_core, for_near):
        for_core[:, :n] = image[...]
        for xi in range(X):
            block = slice(xi * b, (xi + 1) * b)
            for side in range(2):
                r = slice((2 * xi + side) * b, (2 * xi + side + 1) * b)

                @pl.when(at[0] == side)
                def _(block=block, r=r):
                    for_near[:cells, block] = own[:, r]

                @pl.when(at[0] != side)
                def _(block=block, r=r, xi=xi):
                    for_near[cells:, block] = own[:, r]
                    for_core[:, n + xi * b : n + (xi + 1) * b] = other[:, r]

    return dev.call(
        body, "part_cores", [image, other, own], [VMEM] * 3,
        [(cells, n + X * b), (2 * cells, X * b)], [VMEM] * 2,
    )


class Rows:
    def __init__(self, dev, *sources):
        self.X = dev.X
        self.arrays, self.specs, self.cells = [], [], []
        for array, cells, index in sources:
            self.cells.append(cells)
            for xi in range(dev.X):
                self.arrays.append(array)
                self.specs.append(
                    pl.BlockSpec((cells, dev.b), lambda i, at, xi=xi, index=index: index(xi, at))
                )

    def blocks(self, refs):
        return [
            [ref[...] for ref in refs[m * self.X : (m + 1) * self.X]]
            for m in range(len(self.cells))
        ]


def column_blocks(dev, name, rows, cut, width, columns, zs, writes, out_rows):
    X, b = dev.X, dev.b
    top = X // 2
    first, stride = zs
    steps = dev.Z // stride
    nr, nc = len(rows.arrays), len(columns)
    total = sum(rows.cells)

    def body(at, *refs):
        lefts, rights = refs[:nr], refs[nr : nr + nc]
        keep, send, high, low = refs[nr + nc :]

        @pl.when(pl.program_id(0) == 0)
        def _():
            start = 0
            for cells, blocks in zip(rows.cells, rows.blocks(lefts)):
                for xi, block in enumerate(blocks):
                    index = (slice(xi * width, (xi + 1) * width), slice(start, start + cells))
                    turned = block.T[cut * width : (cut + 1) * width]
                    high[index], low[index] = split(turned)
                start += cells

        right = split(jnp.concatenate([ref[...] for ref in rights], 0))
        value = multiply((high[...], low[...]), right)
        zz = stride * pl.program_id(0) + first
        for xi in range(X):
            part = value[xi * width : (xi + 1) * width]
            for side, target in ((at[dev.x_top], keep), (1 - at[dev.x_top], send)):
                for at_rows, condition, result in writes(at, 2 * xi + at[0], zz, part):
                    flag = side == xi // top
                    if condition is not None:
                        flag = jnp.logical_and(flag, condition)

                    @pl.when(flag)
                    def _(target=target, at_rows=at_rows, result=result):
                        target[xi % top, 0, at_rows] = result()

    out = pl.BlockSpec((top, 1, out_rows, b), lambda i, at: (0, i, 0, 0))
    return dev.call(
        body, name, [*rows.arrays, *columns],
        rows.specs
        + [
            pl.BlockSpec((array.shape[0], b), lambda i, at: (0, stride * i + first))
            for array in columns
        ],
        [(top, steps, out_rows, b)] * 2, [out] * 2, grid=(steps,),
        scratch=[pltpu.VMEM((X * width, total), jnp.bfloat16)] * 2,
    )


def project(dev, rows, cut, width, images, zs=(0, 1)):
    writes = lambda at, r, zz, part: [(slice(None), None, lambda: part)]
    return column_blocks(dev, "project", rows, cut, width, images, zs, writes, width)


def lower_rows(dev):
    half = dev.b // 2
    return half // 2 if half % 128 == 0 else half


def overlap(dev, rows, columns, same):
    b = dev.b
    half = b // 2
    more = lower_rows(dev) if same else 0

    def mirrored(part):
        return part[:, half:].T if half % 128 == 0 else part.T[half:]

    def lower(part):
        if more == half:
            return part[half:]
        corner = part[half:, half:]
        return jnp.concatenate([corner[:more], corner[more:]], 1)

    def writes(at, r, zz, part):
        straight = (r <= zz) if same else (at[1] == 0)
        out = [
            (slice(0, half), straight, lambda: part[:half]),
            (slice(0, half), jnp.logical_not(straight), lambda: mirrored(part)),
        ]
        if same:
            out += [
                (slice(half, half + more), r == zz, lambda: lower(part)),
                (slice(half, half + more), r != zz, lambda: jnp.zeros((more, b), jnp.float32)),
            ]
        return out

    return column_blocks(
        dev, "overlap_same" if same else "overlap_mixed", rows, 0, b, columns, (0, 1),
        writes, half + more,
    )


class Sum:
    def __init__(self, rows, *terms):
        self.rows = rows
        self.terms = [(term, [], [], 0) for term in terms]

    def counts(self):
        arrays, xs, zs, _ = self.terms[0]
        n0, n1 = arrays[0].shape[:2]
        return n0 >> len(xs), (n1 * len(arrays)) >> len(zs)


def gather(dev, body, name, sums, pick, arrays_in, out_shapes):
    arrays, slots, shapes = [], [], []
    for total in sums:
        n0, n1 = total.counts()
        if pick == "every":
            n1 = dev.Z - 1
        elif pick is not None:
            n0, n1 = (n0 // 2, n1) if pick[0] == "x" else (n0, n1 // 2)
        for term, _, _, _ in total.terms:
            slots.append(list(range(len(arrays), len(arrays) + len(term))))
            arrays += term
            shapes.append((n0, n1, total.rows, dev.b))
    count, more = len(arrays), len(arrays_in)

    def kernel(at, *refs):
        sources, refs = refs[:count], refs[count:]
        inputs, refs = refs[:more], refs[more:]
        outs, refs = refs[: len(out_shapes)], refs[len(out_shapes) :]
        buffers, sems = refs[:-1], refs[-1]
        waits, k = [], 0
        for total in sums:
            for _, xs, zs, row in total.terms:
                n0, n1, rows, _ = shapes[k]
                xs = [at[bit] for bit in xs]
                zs = [at[bit] for bit in zs]
                if pick == "every":
                    zs = []
                elif pick is not None:
                    (xs if pick[0] == "x" else zs).append(1 - at[pick[1]])
                x_step, z_step = 1 << len(xs), 1 << len(zs)
                x_base = sum((v << i for i, v in enumerate(xs)), 0)
                z_base = sum((v << i for i, v in enumerate(zs)), 0)
                for i in range(n0):
                    for j in range(n1):
                        xi, zi = i * x_step + x_base, j * z_step + z_base
                        if pick == "every":
                            zi = at[len(dev.bits) + 1] ^ (j + 1)
                        target, sem = buffers[k].at[i, j], sems.at[k, i * n1 + j]
                        pair = [sources[slot] for slot in slots[k]]
                        take = zi if len(pair) == 1 else zi // 2
                        copies = [
                            pltpu.make_async_copy(ref.at[xi, take, pl.ds(row, rows)], target, sem)
                            for ref in pair
                        ]
                        if len(pair) == 1:
                            copies[0].start()
                        else:
                            for parity in range(2):
                                pl.when(zi % 2 == parity)(copies[parity].start)
                        waits.append(copies[0])
                k += 1
        for copy in waits:
            copy.wait()
        values, k = [], 0
        for total in sums:
            values.append(buffers[k : k + len(total.terms)])
            k += len(total.terms)
        body(at, values, inputs, outs)

    most = max(shape[0] * shape[1] for shape in shapes)
    return dev.call(
        kernel, name, arrays + arrays_in,
        [pl.BlockSpec(memory_space=pl.ANY)] * count + [VMEM] * more,
        out_shapes, [VMEM] * len(out_shapes),
        scratch=[pltpu.VMEM(shape, jnp.float32) for shape in shapes]
        + [pltpu.SemaphoreType.DMA((len(shapes), most))],
    )


def added(buffers, index):
    total = buffers[0][index]
    for buffer in buffers[1:]:
        total = total + buffer[index]
    return total


def halve(dev, sums, kind, bit):
    n0, n1 = sums[0].counts()
    n0, n1 = (n0 // 2, n1) if kind == "x" else (n0, n1 // 2)
    firsts = [sum(total.rows for total in sums[:k]) for k in range(len(sums) + 1)]

    def body(at, values, inputs, outs):
        for k, total in enumerate(sums):
            for i in range(n0):
                for j in range(n1):
                    outs[0][i, j, firsts[k] : firsts[k + 1]] = added(values[k], (i, j))

    (out,) = gather(
        dev, body, "halve", sums, (kind, bit), [], [(n0, n1, firsts[-1], dev.b)]
    )
    came = dev.swap(out, bit)
    for first, total in zip(firsts, sums):
        total.terms = [
            (arrays, xs + [bit] * (kind == "x"), zs + [bit] * (kind == "z"), row)
            for arrays, xs, zs, row in total.terms
        ] + [((came,), [], [], first)]


def scatter(dev, sums):
    firsts = [sum(total.rows for total in sums[:k]) for k in range(len(sums) + 1)]
    n0 = sums[0].counts()[0]
    others = range(1, dev.Z)

    def body(at, values, inputs, outs):
        for j, out in enumerate(outs):
            for k, total in enumerate(sums):
                for i in range(n0):
                    out[i, 0, firsts[k] : firsts[k + 1]] = added(values[k], (i, j))

    outs = gather(
        dev, body, "scatter", sums, "every", [], [(n0, 1, firsts[-1], dev.b) for _ in others]
    )
    came = [flip(out, "col", 2 * mask) for mask, out in zip(others, outs)]
    for first, total in zip(firsts, sums):
        total.terms = [(arrays, xs, dev.z_bits, row) for arrays, xs, zs, row in total.terms]
        total.terms += [((array,), [], [], first) for array in came]


def finish(dev, total, scale):
    def body(at, values, inputs, outs):
        outs[0][...] = added(values[0], (0, 0)) * scale

    return gather(dev, body, "finish", [total], None, [], [(total.rows, dev.b)])[0]


def assemble_overlap(dev, same, same_half, mixed, mixed_half):
    b = dev.b
    half = b // 2
    more = lower_rows(dev)
    last = len(dev.bits)

    def body(at, same, same_half, mixed, mixed_half, out):
        r, z = at[last], at[last + 1]
        first = pl.multiple_of(at[1] * b, b)
        second = pl.multiple_of((1 - at[1]) * b, b)
        mine = same[:half]

        @pl.when(r < z)
        def _():
            out[pl.ds(first, b)] = jnp.concatenate([mine, same_half[...]], 0)

        @pl.when(r > z)
        def _():
            out[pl.ds(first, b)] = jnp.concatenate([same_half[...], mine], 0).T

        @pl.when(r == z)
        def _():
            lower = same[half:]
            if more < half:
                corner = jnp.concatenate([lower[:, :half], lower[:, half:]], 0)
                lower = jnp.concatenate([mine[:, half:].T, corner], 1)
            out[pl.ds(first, b)] = jnp.concatenate([mine, lower], 0)

        @pl.when(at[1] == 0)
        def _():
            out[pl.ds(second, b)] = jnp.concatenate([mixed[...], mixed_half[...]], 0)

        @pl.when(at[1] == 1)
        def _():
            out[pl.ds(second, b)] = jnp.concatenate([mixed_half[...], mixed[...]], 0).T

    arrays = [same, same_half, mixed, mixed_half]
    return dev.call(
        body, "assemble_overlap", arrays, [VMEM] * 4, [(2 * b, b)], [VMEM]
    )[0]


def rotate(dev, array, rotation):
    cells, orbitals = array.shape
    width = 256 if orbitals % 256 == 0 else orbitals

    def body(at, array, block, out, high, low):
        @pl.when(pl.program_id(0) == 0)
        def _():
            high[...], low[...] = split(array[...])

        out[...] = multiply((high[...], low[...]), split(block[...]))

    return dev.call(
        body, "rotate", [array, rotation],
        [whole(array), pl.BlockSpec((orbitals, width), lambda i, at: (0, i))],
        [array.shape], [pl.BlockSpec((cells, width), lambda i, at: (0, i))],
        grid=(orbitals // width,),
        scratch=[pltpu.VMEM((cells, orbitals), jnp.bfloat16)] * 2,
    )[0]


def local(filtered, hamiltonian_applied, rotation):
    cells, orbitals = filtered.shape
    dev = Device(orbitals)
    R, C, Z, b = dev.R, dev.C, dev.Z, dev.b
    half = b // 2
    scale = 1.0 / (cells * C * R)
    cuts = 2 if b % 256 == 0 else 1
    w = b // cuts

    across = lambda value: flip(value, "col", 1)
    core = lambda value: flip(value, "row", 1)

    def core_pieces(value):
        n = value.shape[0] // 2
        return [core(value[:n]), core(value[n:])]

    own, other = part(dev, "part_orbitals", filtered)
    near = across(other)
    image, image_other = part(dev, "part_images", hamiltonian_applied)
    image_near = across(image_other)
    for_core, for_near = part_cores(dev, own, other, image)
    far = across(for_near)
    own_core, from_core = core(own), core(for_core)
    rotated = rotate(dev, filtered, rotation)

    def reduced_x(rows, keep, send):
        total = Sum(rows, (keep,), (dev.swap(send, dev.x_top),))
        for bit in dev.x_rest:
            halve(dev, [total], "x", bit)
        return total

    near_core = core_pieces(after(near, rotated))
    columns = [own, own_core, near, *near_core]
    this = lambda xi, at: (0, 2 * xi + at[0])
    rows = Rows(dev, *((array, array.shape[0], this) for array in columns))
    same = reduced_x(half + lower_rows(dev), *overlap(dev, rows, columns, True))

    images = [image, from_core, image_near, *core_pieces(after(image_near, dev.last))]
    dev.wait(same)
    even = reduced_x(b, *project(dev, rows, 0, b, images, (0, 2)))
    halve(dev, [same], "z", dev.z_bits[0])
    odd = reduced_x(b, *project(dev, rows, 0, b, images, (1, 2)))
    proj_own = Sum(b)
    proj_own.terms = [(e[0] + o[0], *e[1:]) for e, o in zip(even.terms, odd.terms)]

    far_there = after(far, dev.last)[cells:]
    far_core = core_pieces(far_there)
    dev.wait(even)
    halve(dev, [same], "z", dev.z_bits[1])
    far_rows = Rows(
        dev,
        (other, cells, this),
        (from_core, cells, lambda xi, at: (0, Z + xi)),
        (far, cells, lambda xi, at: (0, xi)),
        *((array, array.shape[0], lambda xi, at: (0, xi)) for array in far_core),
    )
    proj_other = [reduced_x(w, *project(dev, far_rows, 0, w, images))]
    halve(dev, [proj_own], "z", dev.z_bits[0])
    mixed = reduced_x(half, *overlap(dev, far_rows, columns, False))
    for bit in dev.z_bits[2:]:
        halve(dev, [same], "z", bit)
    same = finish(dev, same, scale)
    same_pairs = [
        (i * C + 2 * j + p, j * C + 2 * i + p)
        for i in range(R) for j in range(Z) for p in range(2) if i != j
    ]
    same_half = lax.ppermute(same[:half], ("row", "col"), same_pairs)
    dev.wait(proj_other[0])
    for n in range(1, cuts):
        proj_other.append(reduced_x(w, *project(dev, far_rows, n, w, images)))
    for bit in dev.z_bits[1:]:
        halve(dev, [proj_own], "z", bit)
    halve(dev, [proj_other[0]], "z", dev.z_bits[0])
    scatter(dev, [mixed])
    for total in proj_other[1:]:
        scatter(dev, [total])
    for bit in dev.z_bits[1:]:
        halve(dev, [proj_other[0]], "z", bit)
    mixed = finish(dev, mixed, scale)
    mixed_pairs = [
        (i * C + 2 * j + p, j * C + 2 * i + 1 - p)
        for i in range(R) for j in range(Z) for p in range(2)
    ]
    mixed_half = lax.ppermute(mixed, ("row", "col"), mixed_pairs)

    def assemble(at, values, inputs, outs):
        first = pl.multiple_of(at[1] * b, b)
        second = pl.multiple_of((1 - at[1]) * b, b)
        outs[0][pl.ds(first, b)] = added(values[0], (0, 0)) * scale
        for n in range(cuts):
            outs[0][pl.ds(second + n * w, w)] = added(values[1 + n], (0, 0)) * scale

    (projected,) = gather(
        dev, assemble, "assemble", [proj_own, *proj_other], None, [], [(2 * b, b)]
    )
    intersection = assemble_overlap(dev, same, same_half, mixed, mixed_half)
    return (intersection, projected, rotated)


def solution(mesh):
    return jax.shard_map(
        local,
        mesh=mesh,
        in_specs=(P(("row", "col"), None), P(("row", "col"), None), P()),
        out_specs=(P("row", "col"), P("row", "col"), P(("row", "col"), None)),
        check_vma=False,
    )
```

```python
import jax
import jax.numpy as jnp
from jax import lax
from jax.experimental import pallas as pl
from jax.experimental.pallas import tpu as pltpu
from jax.sharding import PartitionSpec as P


VMEM_LIMIT = 48 * 2**20


def split(value):
    high = value.astype(jnp.bfloat16)
    return high, (value - high.astype(jnp.float32)).astype(jnp.bfloat16)


def multiply(left, right):
    dot = lambda a, b: jnp.dot(a, b, preferred_element_type=jnp.float32)
    (lh, ll), (rh, rl) = left, right
    return dot(lh, rh) + (dot(ll, rh) + dot(lh, rl))


class Device:
    def __init__(self, orbitals):
        self.R, self.C = lax.axis_size("row"), lax.axis_size("col")
        self.X, self.Z = self.R // 2, self.C // 2
        self.b = orbitals // self.C
        r, c = lax.axis_index("row"), lax.axis_index("col")
        self.r, self.c, self.y, self.z = r, c, c % 2, c // 2
        x_bits = self.X.bit_length() - 1
        z_bits = self.Z.bit_length() - 1
        self.bits = [r % 2, self.y]
        self.bits += [(r >> (1 + i)) & 1 for i in range(x_bits)]
        self.bits += [(self.z >> i) & 1 for i in range(z_bits)]
        self.x_top = 1 + x_bits
        self.x_rest = list(range(2, 1 + x_bits))
        self.z_bits = list(range(2 + x_bits, 2 + x_bits + z_bits))
        self.at = jnp.stack(self.bits + [r, self.z]).astype(jnp.int32)
        self.last, self.waits = None, []

    def axis_bit(self, bit):
        if bit < self.z_bits[0]:
            return "row", bit - 1
        return "col", bit - self.z_bits[0] + 1

    def swap(self, value, bit):
        axis, shift = self.axis_bit(bit)
        return flip(value, axis, 1 << shift)

    def wait(self, total):
        self.waits += total.terms[-1][0]

    def call(self, body, name, arrays, in_specs, out_shapes, out_specs, grid=(), scratch=()):
        after = ([] if self.last is None else [self.last]) + self.waits
        self.waits = []
        count = len(arrays)

        def ordered(at, *refs):
            body(at, *refs[:count], *refs[count + len(after) :])

        outs = pl.pallas_call(
            ordered,
            name=name,
            out_shape=[jax.ShapeDtypeStruct(s, jnp.float32) for s in out_shapes],
            grid_spec=pltpu.PrefetchScalarGridSpec(
                num_scalar_prefetch=1,
                grid=grid,
                in_specs=list(in_specs) + [pl.BlockSpec(memory_space=pl.ANY)] * len(after),
                out_specs=list(out_specs),
                scratch_shapes=list(scratch),
            ),
            compiler_params=pltpu.CompilerParams(vmem_limit_bytes=VMEM_LIMIT),
            cost_estimate=pl.CostEstimate(flops=0, bytes_accessed=0, transcendentals=0),
        )(self.at, *arrays, *after)
        self.last = outs[0]
        return outs


def flip(value, axis, mask):
    count = lax.axis_size(axis)
    return lax.ppermute(value, axis, [(i, i ^ mask) for i in range(count)])


VMEM = pl.BlockSpec(memory_space=pltpu.VMEM)


def after(value, other):
    return lax.optimization_barrier((value, other))[0]


def whole(array):
    return pl.BlockSpec(array.shape, lambda i, at: (0,) * array.ndim)


def part(dev, name, array):
    cells, b = array.shape[0], dev.b

    def body(at, source, own, other):
        even, odd = source[:, :b], source[:, b:]
        first = at[1] == 0
        own[...] = jnp.where(first, even, odd)
        other[...] = jnp.where(first, odd, even)

    block = lambda width: pl.BlockSpec((cells, width), lambda i, at: (0, i))
    return dev.call(
        body, name, [array], [block(2 * b)], [(cells, dev.R * b)] * 2,
        [block(b)] * 2, grid=(dev.R,),
    )


def part_cores(dev, own, other, image):
    cells, b, X, Z = own.shape[0], dev.b, dev.X, dev.Z
    n = Z * b

    def body(at, image, other, own, for_core, for_near):
        for_core[:, :n] = image[...]
        for xi in range(X):
            block = slice(xi * b, (xi + 1) * b)
            for side in range(2):
                r = slice((2 * xi + side) * b, (2 * xi + side + 1) * b)

                @pl.when(at[0] == side)
                def _(block=block, r=r):
                    for_near[:cells, block] = own[:, r]

                @pl.when(at[0] != side)
                def _(block=block, r=r, xi=xi):
                    for_near[cells:, block] = own[:, r]
                    for_core[:, n + xi * b : n + (xi + 1) * b] = other[:, r]

    return dev.call(
        body, "part_cores", [image, other, own], [VMEM] * 3,
        [(cells, n + X * b), (2 * cells, X * b)], [VMEM] * 2,
    )


class Rows:
    def __init__(self, dev, *sources):
        self.X = dev.X
        self.arrays, self.specs, self.cells = [], [], []
        for array, cells, index in sources:
            self.cells.append(cells)
            for xi in range(dev.X):
                self.arrays.append(array)
                self.specs.append(
                    pl.BlockSpec((cells, dev.b), lambda i, at, xi=xi, index=index: index(xi, at))
                )

    def blocks(self, refs):
        return [
            [ref[...] for ref in refs[m * self.X : (m + 1) * self.X]]
            for m in range(len(self.cells))
        ]


def column_blocks(dev, name, rows, cut, width, columns, zs, writes, out_rows):
    X, b = dev.X, dev.b
    top = X // 2
    first, stride = zs
    steps = dev.Z // stride
    nr, nc = len(rows.arrays), len(columns)
    total = sum(rows.cells)

    def body(at, *refs):
        lefts, rights = refs[:nr], refs[nr : nr + nc]
        keep, send, high, low = refs[nr + nc :]

        @pl.when(pl.program_id(0) == 0)
        def _():
            start = 0
            for cells, blocks in zip(rows.cells, rows.blocks(lefts)):
                for xi, block in enumerate(blocks):
                    index = (slice(xi * width, (xi + 1) * width), slice(start, start + cells))
                    turned = block.T[cut * width : (cut + 1) * width]
                    high[index], low[index] = split(turned)
                start += cells

        right = split(jnp.concatenate([ref[...] for ref in rights], 0))
        value = multiply((high[...], low[...]), right)
        zz = stride * pl.program_id(0) + first
        for xi in range(X):
            part = value[xi * width : (xi + 1) * width]
            for side, target in ((at[dev.x_top], keep), (1 - at[dev.x_top], send)):
                for at_rows, condition, result in writes(at, 2 * xi + at[0], zz, part):
                    flag = side == xi // top
                    if condition is not None:
                        flag = jnp.logical_and(flag, condition)

                    @pl.when(flag)
                    def _(target=target, at_rows=at_rows, result=result):
                        target[xi % top, 0, at_rows] = result()

    out = pl.BlockSpec((top, 1, out_rows, b), lambda i, at: (0, i, 0, 0))
    return dev.call(
        body, name, [*rows.arrays, *columns],
        rows.specs
        + [
            pl.BlockSpec((array.shape[0], b), lambda i, at: (0, stride * i + first))
            for array in columns
        ],
        [(top, steps, out_rows, b)] * 2, [out] * 2, grid=(steps,),
        scratch=[pltpu.VMEM((X * width, total), jnp.bfloat16)] * 2,
    )


def project(dev, rows, cut, width, images, zs=(0, 1)):
    writes = lambda at, r, zz, part: [(slice(None), None, lambda: part)]
    return column_blocks(dev, "project", rows, cut, width, images, zs, writes, width)


def lower_rows(dev):
    half = dev.b // 2
    return half // 2 if half % 128 == 0 else half


def overlap(dev, rows, columns, same):
    b = dev.b
    half = b // 2
    more = lower_rows(dev) if same else 0

    def mirrored(part):
        return part[:, half:].T if half % 128 == 0 else part.T[half:]

    def lower(part):
        if more == half:
            return part[half:]
        corner = part[half:, half:]
        return jnp.concatenate([corner[:more], corner[more:]], 1)

    def writes(at, r, zz, part):
        straight = (r <= zz) if same else (at[1] == 0)
        out = [
            (slice(0, half), straight, lambda: part[:half]),
            (slice(0, half), jnp.logical_not(straight), lambda: mirrored(part)),
        ]
        if same:
            out += [
                (slice(half, half + more), r == zz, lambda: lower(part)),
                (slice(half, half + more), r != zz, lambda: jnp.zeros((more, b), jnp.float32)),
            ]
        return out

    return column_blocks(
        dev, "overlap_same" if same else "overlap_mixed", rows, 0, b, columns, (0, 1),
        writes, half + more,
    )


class Sum:
    def __init__(self, rows, *terms):
        self.rows = rows
        self.terms = [(term, [], [], 0) for term in terms]

    def counts(self):
        arrays, xs, zs, _ = self.terms[0]
        n0, n1 = arrays[0].shape[:2]
        return n0 >> len(xs), (n1 * len(arrays)) >> len(zs)


def gather(dev, body, name, sums, pick, arrays_in, out_shapes):
    arrays, slots, shapes = [], [], []
    for total in sums:
        n0, n1 = total.counts()
        if pick == "every":
            n1 = dev.Z - 1
        elif pick is not None:
            n0, n1 = (n0 // 2, n1) if pick[0] == "x" else (n0, n1 // 2)
        for term, _, _, _ in total.terms:
            slots.append(list(range(len(arrays), len(arrays) + len(term))))
            arrays += term
            shapes.append((n0, n1, total.rows, dev.b))
    count, more = len(arrays), len(arrays_in)

    def kernel(at, *refs):
        sources, refs = refs[:count], refs[count:]
        inputs, refs = refs[:more], refs[more:]
        outs, refs = refs[: len(out_shapes)], refs[len(out_shapes) :]
        buffers, sems = refs[:-1], refs[-1]
        waits, k = [], 0
        for total in sums:
            for _, xs, zs, row in total.terms:
                n0, n1, rows, _ = shapes[k]
                xs = [at[bit] for bit in xs]
                zs = [at[bit] for bit in zs]
                if pick == "every":
                    zs = []
                elif pick is not None:
                    (xs if pick[0] == "x" else zs).append(1 - at[pick[1]])
                x_step, z_step = 1 << len(xs), 1 << len(zs)
                x_base = sum((v << i for i, v in enumerate(xs)), 0)
                z_base = sum((v << i for i, v in enumerate(zs)), 0)
                for i in range(n0):
                    for j in range(n1):
                        xi, zi = i * x_step + x_base, j * z_step + z_base
                        if pick == "every":
                            zi = at[len(dev.bits) + 1] ^ (j + 1)
                        target, sem = buffers[k].at[i, j], sems.at[k, i * n1 + j]
                        pair = [sources[slot] for slot in slots[k]]
                        take = zi if len(pair) == 1 else zi // 2
                        copies = [
                            pltpu.make_async_copy(ref.at[xi, take, pl.ds(row, rows)], target, sem)
                            for ref in pair
                        ]
                        if len(pair) == 1:
                            copies[0].start()
                        else:
                            for parity in range(2):
                                pl.when(zi % 2 == parity)(copies[parity].start)
                        waits.append(copies[0])
                k += 1
        for copy in waits:
            copy.wait()
        values, k = [], 0
        for total in sums:
            values.append(buffers[k : k + len(total.terms)])
            k += len(total.terms)
        body(at, values, inputs, outs)

    most = max(shape[0] * shape[1] for shape in shapes)
    return dev.call(
        kernel, name, arrays + arrays_in,
        [pl.BlockSpec(memory_space=pl.ANY)] * count + [VMEM] * more,
        out_shapes, [VMEM] * len(out_shapes),
        scratch=[pltpu.VMEM(shape, jnp.float32) for shape in shapes]
        + [pltpu.SemaphoreType.DMA((len(shapes), most))],
    )


def added(buffers, index):
    total = buffers[0][index]
    for buffer in buffers[1:]:
        total = total + buffer[index]
    return total


def halve(dev, sums, kind, bit):
    n0, n1 = sums[0].counts()
    n0, n1 = (n0 // 2, n1) if kind == "x" else (n0, n1 // 2)
    firsts = [sum(total.rows for total in sums[:k]) for k in range(len(sums) + 1)]

    def body(at, values, inputs, outs):
        for k, total in enumerate(sums):
            for i in range(n0):
                for j in range(n1):
                    outs[0][i, j, firsts[k] : firsts[k + 1]] = added(values[k], (i, j))

    (out,) = gather(
        dev, body, "halve", sums, (kind, bit), [], [(n0, n1, firsts[-1], dev.b)]
    )
    came = dev.swap(out, bit)
    for first, total in zip(firsts, sums):
        total.terms = [
            (arrays, xs + [bit] * (kind == "x"), zs + [bit] * (kind == "z"), row)
            for arrays, xs, zs, row in total.terms
        ] + [((came,), [], [], first)]


def scatter(dev, sums):
    firsts = [sum(total.rows for total in sums[:k]) for k in range(len(sums) + 1)]
    n0 = sums[0].counts()[0]
    others = range(1, dev.Z)

    def body(at, values, inputs, outs):
        for j, out in enumerate(outs):
            for k, total in enumerate(sums):
                for i in range(n0):
                    out[i, 0, firsts[k] : firsts[k + 1]] = added(values[k], (i, j))

    outs = gather(
        dev, body, "scatter", sums, "every", [], [(n0, 1, firsts[-1], dev.b) for _ in others]
    )
    came = [flip(out, "col", 2 * mask) for mask, out in zip(others, outs)]
    for first, total in zip(firsts, sums):
        total.terms = [(arrays, xs, dev.z_bits, row) for arrays, xs, zs, row in total.terms]
        total.terms += [((array,), [], [], first) for array in came]


def finish(dev, total, scale):
    def body(at, values, inputs, outs):
        outs[0][...] = added(values[0], (0, 0)) * scale

    return gather(dev, body, "finish", [total], None, [], [(total.rows, dev.b)])[0]


def assemble_overlap(dev, same, same_half, mixed, mixed_half):
    b = dev.b
    half = b // 2
    more = lower_rows(dev)
    last = len(dev.bits)

    def body(at, same, same_half, mixed, mixed_half, out):
        r, z = at[last], at[last + 1]
        first = pl.multiple_of(at[1] * b, b)
        second = pl.multiple_of((1 - at[1]) * b, b)
        mine = same[:half]

        @pl.when(r < z)
        def _():
            out[pl.ds(first, b)] = jnp.concatenate([mine, same_half[...]], 0)

        @pl.when(r > z)
        def _():
            out[pl.ds(first, b)] = jnp.concatenate([same_half[...], mine], 0).T

        @pl.when(r == z)
        def _():
            lower = same[half:]
            if more < half:
                corner = jnp.concatenate([lower[:, :half], lower[:, half:]], 0)
                lower = jnp.concatenate([mine[:, half:].T, corner], 1)
            out[pl.ds(first, b)] = jnp.concatenate([mine, lower], 0)

        @pl.when(at[1] == 0)
        def _():
            out[pl.ds(second, b)] = jnp.concatenate([mixed[...], mixed_half[...]], 0)

        @pl.when(at[1] == 1)
        def _():
            out[pl.ds(second, b)] = jnp.concatenate([mixed_half[...], mixed[...]], 0).T

    arrays = [same, same_half, mixed, mixed_half]
    return dev.call(
        body, "assemble_overlap", arrays, [VMEM] * 4, [(2 * b, b)], [VMEM]
    )[0]


def rotate(dev, array, rotation):
    cells, orbitals = array.shape
    width = 256 if orbitals % 256 == 0 else orbitals

    def body(at, array, block, out, high, low):
        @pl.when(pl.program_id(0) == 0)
        def _():
            high[...], low[...] = split(array[...])

        out[...] = multiply((high[...], low[...]), split(block[...]))

    return dev.call(
        body, "rotate", [array, rotation],
        [whole(array), pl.BlockSpec((orbitals, width), lambda i, at: (0, i))],
        [array.shape], [pl.BlockSpec((cells, width), lambda i, at: (0, i))],
        grid=(orbitals // width,),
        scratch=[pltpu.VMEM((cells, orbitals), jnp.bfloat16)] * 2,
    )[0]


def local(filtered, hamiltonian_applied, rotation):
    cells, orbitals = filtered.shape
    dev = Device(orbitals)
    R, C, Z, b = dev.R, dev.C, dev.Z, dev.b
    half = b // 2
    scale = 1.0 / (cells * C * R)
    cuts = 2 if b % 256 == 0 else 1
    w = b // cuts

    across = lambda value: flip(value, "col", 1)
    core = lambda value: flip(value, "row", 1)

    def core_pieces(value, *ends):
        ends = (*ends, value.shape[0])
        return [core(value[first:end]) for first, end in zip((0, *ends), ends)]

    own, other = part(dev, "part_orbitals", filtered)
    near = across(other)
    image, image_other = part(dev, "part_images", hamiltonian_applied)
    image_near = across(image_other)
    for_core, for_near = part_cores(dev, own, other, image)
    far = across(for_near)
    own_core, from_core = core(own), core(for_core)
    rotated = rotate(dev, filtered, rotation)

    def reduced_x(rows, keep, send):
        total = Sum(rows, (keep,), (dev.swap(send, dev.x_top),))
        for bit in dev.x_rest:
            halve(dev, [total], "x", bit)
        return total

    near_core = core_pieces(after(near, rotated), cells // 2)
    columns = [own, own_core, near, *near_core]
    this = lambda xi, at: (0, 2 * xi + at[0])
    rows = Rows(dev, *((array, array.shape[0], this) for array in columns))
    same = reduced_x(half + lower_rows(dev), *overlap(dev, rows, columns, True))

    images = [image, from_core, image_near, *core_pieces(after(image_near, dev.last), cells * 3 // 8, cells * 11 // 16)]
    even = reduced_x(b, *project(dev, rows, 0, b, images, (0, 2)))
    halve(dev, [same], "z", dev.z_bits[0])
    odd = reduced_x(b, *project(dev, rows, 0, b, images, (1, 2)))
    proj_own = Sum(b)
    proj_own.terms = [(e[0] + o[0], *e[1:]) for e, o in zip(even.terms, odd.terms)]

    far_there = after(far, dev.last)[cells:]
    far_core = core_pieces(far_there, cells // 2)
    dev.wait(even)
    far_rows = Rows(
        dev,
        (other, cells, this),
        (from_core, cells, lambda xi, at: (0, Z + xi)),
        (far, cells, lambda xi, at: (0, xi)),
        *((array, array.shape[0], lambda xi, at: (0, xi)) for array in far_core),
    )
    mixed = reduced_x(half, *overlap(dev, far_rows, columns, False))
    halve(dev, [same], "z", dev.z_bits[1])
    halve(dev, [proj_own], "z", dev.z_bits[0])
    proj_other = [reduced_x(w, *project(dev, far_rows, 0, w, images))]
    for bit in dev.z_bits[2:]:
        halve(dev, [same], "z", bit)
    same = finish(dev, same, scale)
    same_pairs = [
        (i * C + 2 * j + p, j * C + 2 * i + p)
        for i in range(R) for j in range(Z) for p in range(2) if i != j
    ]
    same_half = lax.ppermute(same[:half], ("row", "col"), same_pairs)
    halve(dev, [mixed], "z", dev.z_bits[0])
    for n in range(1, cuts):
        proj_other.append(reduced_x(w, *project(dev, far_rows, n, w, images)))
    dev.waits.append(same_half)
    for bit in dev.z_bits[1:]:
        halve(dev, [proj_own], "z", bit)
    for bit in dev.z_bits[1:]:
        halve(dev, [mixed], "z", bit)
    halve(dev, [proj_other[0]], "z", dev.z_bits[0])
    for total in proj_other[1:]:
        halve(dev, [total], "z", dev.z_bits[0])
    dev.wait(proj_own)
    for bit in dev.z_bits[1:]:
        halve(dev, [proj_other[0]], "z", bit)
    mixed = finish(dev, mixed, scale)
    mixed_pairs = [
        (i * C + 2 * j + p, j * C + 2 * i + 1 - p)
        for i in range(R) for j in range(Z) for p in range(2)
    ]
    mixed_half = lax.ppermute(mixed, ("row", "col"), mixed_pairs)
    for total in proj_other[1:]:
        for bit in dev.z_bits[1:]:
            halve(dev, [total], "z", bit)
    intersection = assemble_overlap(dev, same, same_half, mixed, mixed_half)

    def assemble(at, values, inputs, outs):
        first = pl.multiple_of(at[1] * b, b)
        second = pl.multiple_of((1 - at[1]) * b, b)
        outs[0][pl.ds(first, b)] = added(values[0], (0, 0)) * scale
        for n in range(cuts):
            outs[0][pl.ds(second + n * w, w)] = added(values[1 + n], (0, 0)) * scale

    (projected,) = gather(
        dev, assemble, "assemble", [proj_own, *proj_other], None, [], [(2 * b, b)]
    )
    return (intersection, projected, rotated)


def solution(mesh):
    return jax.shard_map(
        local,
        mesh=mesh,
        in_specs=(P(("row", "col"), None), P(("row", "col"), None), P()),
        out_specs=(P("row", "col"), P("row", "col"), P(("row", "col"), None)),
        check_vma=False,
    )
```

```python
import jax
import jax.numpy as jnp
from jax import lax
from jax.experimental import pallas as pl
from jax.experimental.pallas import tpu as pltpu
from jax.sharding import PartitionSpec as P


VMEM_LIMIT = 48 * 2**20


def split(value):
    high = value.astype(jnp.bfloat16)
    return high, (value - high.astype(jnp.float32)).astype(jnp.bfloat16)


def multiply(left, right):
    dot = lambda a, b: jnp.dot(a, b, preferred_element_type=jnp.float32)
    (lh, ll), (rh, rl) = left, right
    return dot(lh, rh) + (dot(ll, rh) + dot(lh, rl))


class Device:
    def __init__(self, orbitals):
        self.R, self.C = lax.axis_size("row"), lax.axis_size("col")
        self.X, self.Z = self.R // 2, self.C // 2
        self.b = orbitals // self.C
        r, c = lax.axis_index("row"), lax.axis_index("col")
        self.r, self.c, self.y, self.z = r, c, c % 2, c // 2
        x_bits = self.X.bit_length() - 1
        z_bits = self.Z.bit_length() - 1
        self.bits = [r % 2, self.y]
        self.bits += [(r >> (1 + i)) & 1 for i in range(x_bits)]
        self.bits += [(self.z >> i) & 1 for i in range(z_bits)]
        self.x_top = 1 + x_bits
        self.x_rest = list(range(2, 1 + x_bits))
        self.z_bits = list(range(2 + x_bits, 2 + x_bits + z_bits))
        self.at = jnp.stack(self.bits + [r, self.z]).astype(jnp.int32)
        self.last, self.waits = None, []

    def axis_bit(self, bit):
        if bit < self.z_bits[0]:
            return "row", bit - 1
        return "col", bit - self.z_bits[0] + 1

    def swap(self, value, bit):
        axis, shift = self.axis_bit(bit)
        return flip(value, axis, 1 << shift)

    def wait(self, total):
        self.waits += total.terms[-1][0]

    def call(self, body, name, arrays, in_specs, out_shapes, out_specs, grid=(), scratch=()):
        after = ([] if self.last is None else [self.last]) + self.waits
        self.waits = []
        count = len(arrays)

        def ordered(at, *refs):
            body(at, *refs[:count], *refs[count + len(after) :])

        outs = pl.pallas_call(
            ordered,
            name=name,
            out_shape=[jax.ShapeDtypeStruct(s, jnp.float32) for s in out_shapes],
            grid_spec=pltpu.PrefetchScalarGridSpec(
                num_scalar_prefetch=1,
                grid=grid,
                in_specs=list(in_specs) + [pl.BlockSpec(memory_space=pl.ANY)] * len(after),
                out_specs=list(out_specs),
                scratch_shapes=list(scratch),
            ),
            compiler_params=pltpu.CompilerParams(vmem_limit_bytes=VMEM_LIMIT),
            cost_estimate=pl.CostEstimate(flops=0, bytes_accessed=0, transcendentals=0),
        )(self.at, *arrays, *after)
        self.last = outs[0]
        return outs


def flip(value, axis, mask):
    count = lax.axis_size(axis)
    return lax.ppermute(value, axis, [(i, i ^ mask) for i in range(count)])


VMEM = pl.BlockSpec(memory_space=pltpu.VMEM)


def after(value, other):
    return lax.optimization_barrier((value, other))[0]


def whole(array):
    return pl.BlockSpec(array.shape, lambda i, at: (0,) * array.ndim)


def part(dev, name, array):
    cells, b = array.shape[0], dev.b

    def body(at, source, own, other):
        even, odd = source[:, :b], source[:, b:]
        first = at[1] == 0
        own[...] = jnp.where(first, even, odd)
        other[...] = jnp.where(first, odd, even)

    block = lambda width: pl.BlockSpec((cells, width), lambda i, at: (0, i))
    return dev.call(
        body, name, [array], [block(2 * b)], [(cells, dev.R * b)] * 2,
        [block(b)] * 2, grid=(dev.R,),
    )


def part_cores(dev, own, other, image):
    cells, b, X, Z = own.shape[0], dev.b, dev.X, dev.Z
    n = Z * b

    def body(at, image, other, own, for_core, for_near):
        for_core[:, :n] = image[...]
        for xi in range(X):
            block = slice(xi * b, (xi + 1) * b)
            for side in range(2):
                r = slice((2 * xi + side) * b, (2 * xi + side + 1) * b)

                @pl.when(at[0] == side)
                def _(block=block, r=r):
                    for_near[:cells, block] = own[:, r]

                @pl.when(at[0] != side)
                def _(block=block, r=r, xi=xi):
                    for_near[cells:, block] = own[:, r]
                    for_core[:, n + xi * b : n + (xi + 1) * b] = other[:, r]

    return dev.call(
        body, "part_cores", [image, other, own], [VMEM] * 3,
        [(cells, n + X * b), (2 * cells, X * b)], [VMEM] * 2,
    )


class Rows:
    def __init__(self, dev, *sources):
        self.X = dev.X
        self.arrays, self.specs, self.cells = [], [], []
        for array, cells, index in sources:
            self.cells.append(cells)
            for xi in range(dev.X):
                self.arrays.append(array)
                self.specs.append(
                    pl.BlockSpec((cells, dev.b), lambda i, at, xi=xi, index=index: index(xi, at))
                )

    def blocks(self, refs):
        return [
            [ref[...] for ref in refs[m * self.X : (m + 1) * self.X]]
            for m in range(len(self.cells))
        ]


def column_blocks(dev, name, rows, cut, width, columns, zs, writes, out_rows):
    X, b = dev.X, dev.b
    top = X // 2
    first, stride = zs
    steps = dev.Z // stride
    nr, nc = len(rows.arrays), len(columns)
    total = sum(rows.cells)

    def body(at, *refs):
        lefts, rights = refs[:nr], refs[nr : nr + nc]
        keep, send, high, low = refs[nr + nc :]

        @pl.when(pl.program_id(0) == 0)
        def _():
            start = 0
            for cells, blocks in zip(rows.cells, rows.blocks(lefts)):
                for xi, block in enumerate(blocks):
                    index = (slice(xi * width, (xi + 1) * width), slice(start, start + cells))
                    turned = block.T[cut * width : (cut + 1) * width]
                    high[index], low[index] = split(turned)
                start += cells

        right = split(jnp.concatenate([ref[...] for ref in rights], 0))
        value = multiply((high[...], low[...]), right)
        zz = stride * pl.program_id(0) + first
        for xi in range(X):
            part = value[xi * width : (xi + 1) * width]
            for side, target in ((at[dev.x_top], keep), (1 - at[dev.x_top], send)):
                for at_rows, condition, result in writes(at, 2 * xi + at[0], zz, part):
                    flag = side == xi // top
                    if condition is not None:
                        flag = jnp.logical_and(flag, condition)

                    @pl.when(flag)
                    def _(target=target, at_rows=at_rows, result=result):
                        target[xi % top, 0, at_rows] = result()

    out = pl.BlockSpec((top, 1, out_rows, b), lambda i, at: (0, i, 0, 0))
    return dev.call(
        body, name, [*rows.arrays, *columns],
        rows.specs
        + [
            pl.BlockSpec((array.shape[0], b), lambda i, at: (0, stride * i + first))
            for array in columns
        ],
        [(top, steps, out_rows, b)] * 2, [out] * 2, grid=(steps,),
        scratch=[pltpu.VMEM((X * width, total), jnp.bfloat16)] * 2,
    )


def project(dev, rows, cut, width, images, zs=(0, 1)):
    writes = lambda at, r, zz, part: [(slice(None), None, lambda: part)]
    return column_blocks(dev, "project", rows, cut, width, images, zs, writes, width)


def lower_rows(dev):
    half = dev.b // 2
    return half // 2 if half % 128 == 0 else half


def overlap(dev, rows, columns, same):
    b = dev.b
    half = b // 2
    more = lower_rows(dev) if same else 0

    def mirrored(part):
        return part[:, half:].T if half % 128 == 0 else part.T[half:]

    def lower(part):
        if more == half:
            return part[half:]
        corner = part[half:, half:]
        return jnp.concatenate([corner[:more], corner[more:]], 1)

    def writes(at, r, zz, part):
        straight = (r <= zz) if same else (at[1] == 0)
        out = [
            (slice(0, half), straight, lambda: part[:half]),
            (slice(0, half), jnp.logical_not(straight), lambda: mirrored(part)),
        ]
        if same:
            out += [
                (slice(half, half + more), r == zz, lambda: lower(part)),
                (slice(half, half + more), r != zz, lambda: jnp.zeros((more, b), jnp.float32)),
            ]
        return out

    return column_blocks(
        dev, "overlap_same" if same else "overlap_mixed", rows, 0, b, columns, (0, 1),
        writes, half + more,
    )


class Sum:
    def __init__(self, rows, *terms):
        self.rows = rows
        self.terms = [(term, [], [], 0) for term in terms]

    def counts(self):
        arrays, xs, zs, _ = self.terms[0]
        n0, n1 = arrays[0].shape[:2]
        return n0 >> len(xs), (n1 * len(arrays)) >> len(zs)


def gather(dev, body, name, sums, pick, arrays_in, out_shapes):
    arrays, slots, shapes = [], [], []
    for total in sums:
        n0, n1 = total.counts()
        if pick == "every":
            n1 = dev.Z - 1
        elif pick is not None:
            n0, n1 = (n0 // 2, n1) if pick[0] == "x" else (n0, n1 // 2)
        for term, _, _, _ in total.terms:
            slots.append(list(range(len(arrays), len(arrays) + len(term))))
            arrays += term
            shapes.append((n0, n1, total.rows, dev.b))
    count, more = len(arrays), len(arrays_in)

    def kernel(at, *refs):
        sources, refs = refs[:count], refs[count:]
        inputs, refs = refs[:more], refs[more:]
        outs, refs = refs[: len(out_shapes)], refs[len(out_shapes) :]
        buffers, sems = refs[:-1], refs[-1]
        waits, k = [], 0
        for total in sums:
            for _, xs, zs, row in total.terms:
                n0, n1, rows, _ = shapes[k]
                xs = [at[bit] for bit in xs]
                zs = [at[bit] for bit in zs]
                if pick == "every":
                    zs = []
                elif pick is not None:
                    (xs if pick[0] == "x" else zs).append(1 - at[pick[1]])
                x_step, z_step = 1 << len(xs), 1 << len(zs)
                x_base = sum((v << i for i, v in enumerate(xs)), 0)
                z_base = sum((v << i for i, v in enumerate(zs)), 0)
                for i in range(n0):
                    for j in range(n1):
                        xi, zi = i * x_step + x_base, j * z_step + z_base
                        if pick == "every":
                            zi = at[len(dev.bits) + 1] ^ (j + 1)
                        target, sem = buffers[k].at[i, j], sems.at[k, i * n1 + j]
                        pair = [sources[slot] for slot in slots[k]]
                        take = zi if len(pair) == 1 else zi // 2
                        copies = [
                            pltpu.make_async_copy(ref.at[xi, take, pl.ds(row, rows)], target, sem)
                            for ref in pair
                        ]
                        if len(pair) == 1:
                            copies[0].start()
                        else:
                            for parity in range(2):
                                pl.when(zi % 2 == parity)(copies[parity].start)
                        waits.append(copies[0])
                k += 1
        for copy in waits:
            copy.wait()
        values, k = [], 0
        for total in sums:
            values.append(buffers[k : k + len(total.terms)])
            k += len(total.terms)
        body(at, values, inputs, outs)

    most = max(shape[0] * shape[1] for shape in shapes)
    return dev.call(
        kernel, name, arrays + arrays_in,
        [pl.BlockSpec(memory_space=pl.ANY)] * count + [VMEM] * more,
        out_shapes, [VMEM] * len(out_shapes),
        scratch=[pltpu.VMEM(shape, jnp.float32) for shape in shapes]
        + [pltpu.SemaphoreType.DMA((len(shapes), most))],
    )


def added(buffers, index):
    total = buffers[0][index]
    for buffer in buffers[1:]:
        total = total + buffer[index]
    return total


def halve(dev, sums, kind, bit):
    n0, n1 = sums[0].counts()
    n0, n1 = (n0 // 2, n1) if kind == "x" else (n0, n1 // 2)
    firsts = [sum(total.rows for total in sums[:k]) for k in range(len(sums) + 1)]

    def body(at, values, inputs, outs):
        for k, total in enumerate(sums):
            for i in range(n0):
                for j in range(n1):
                    outs[0][i, j, firsts[k] : firsts[k + 1]] = added(values[k], (i, j))

    (out,) = gather(
        dev, body, "halve", sums, (kind, bit), [], [(n0, n1, firsts[-1], dev.b)]
    )
    came = dev.swap(out, bit)
    for first, total in zip(firsts, sums):
        total.terms = [
            (arrays, xs + [bit] * (kind == "x"), zs + [bit] * (kind == "z"), row)
            for arrays, xs, zs, row in total.terms
        ] + [((came,), [], [], first)]


def scatter(dev, sums):
    firsts = [sum(total.rows for total in sums[:k]) for k in range(len(sums) + 1)]
    n0 = sums[0].counts()[0]
    others = range(1, dev.Z)

    def body(at, values, inputs, outs):
        for j, out in enumerate(outs):
            for k, total in enumerate(sums):
                for i in range(n0):
                    out[i, 0, firsts[k] : firsts[k + 1]] = added(values[k], (i, j))

    outs = gather(
        dev, body, "scatter", sums, "every", [], [(n0, 1, firsts[-1], dev.b) for _ in others]
    )
    came = [flip(out, "col", 2 * mask) for mask, out in zip(others, outs)]
    for first, total in zip(firsts, sums):
        total.terms = [(arrays, xs, dev.z_bits, row) for arrays, xs, zs, row in total.terms]
        total.terms += [((array,), [], [], first) for array in came]


def finish(dev, total, scale):
    def body(at, values, inputs, outs):
        outs[0][...] = added(values[0], (0, 0)) * scale

    return gather(dev, body, "finish", [total], None, [], [(total.rows, dev.b)])[0]


def assemble_overlap(dev, same, same_half, mixed, mixed_half):
    b = dev.b
    half = b // 2
    more = lower_rows(dev)
    last = len(dev.bits)

    def body(at, same, same_half, mixed, mixed_half, out):
        r, z = at[last], at[last + 1]
        first = pl.multiple_of(at[1] * b, b)
        second = pl.multiple_of((1 - at[1]) * b, b)
        mine = same[:half]

        @pl.when(r < z)
        def _():
            out[pl.ds(first, b)] = jnp.concatenate([mine, same_half[...]], 0)

        @pl.when(r > z)
        def _():
            out[pl.ds(first, b)] = jnp.concatenate([same_half[...], mine], 0).T

        @pl.when(r == z)
        def _():
            lower = same[half:]
            if more < half:
                corner = jnp.concatenate([lower[:, :half], lower[:, half:]], 0)
                lower = jnp.concatenate([mine[:, half:].T, corner], 1)
            out[pl.ds(first, b)] = jnp.concatenate([mine, lower], 0)

        @pl.when(at[1] == 0)
        def _():
            out[pl.ds(second, b)] = jnp.concatenate([mixed[...], mixed_half[...]], 0)

        @pl.when(at[1] == 1)
        def _():
            out[pl.ds(second, b)] = jnp.concatenate([mixed_half[...], mixed[...]], 0).T

    arrays = [same, same_half, mixed, mixed_half]
    return dev.call(
        body, "assemble_overlap", arrays, [VMEM] * 4, [(2 * b, b)], [VMEM]
    )[0]


def rotate(dev, array, rotation):
    cells, orbitals = array.shape
    width = 256 if orbitals % 256 == 0 else orbitals

    def body(at, array, block, out, high, low):
        @pl.when(pl.program_id(0) == 0)
        def _():
            high[...], low[...] = split(array[...])

        out[...] = multiply((high[...], low[...]), split(block[...]))

    return dev.call(
        body, "rotate", [array, rotation],
        [whole(array), pl.BlockSpec((orbitals, width), lambda i, at: (0, i))],
        [array.shape], [pl.BlockSpec((cells, width), lambda i, at: (0, i))],
        grid=(orbitals // width,),
        scratch=[pltpu.VMEM((cells, orbitals), jnp.bfloat16)] * 2,
    )[0]


def local(filtered, hamiltonian_applied, rotation):
    cells, orbitals = filtered.shape
    dev = Device(orbitals)
    R, C, Z, b = dev.R, dev.C, dev.Z, dev.b
    half = b // 2
    scale = 1.0 / (cells * C * R)
    cuts = 2 if b % 256 == 0 else 1
    w = b // cuts

    across = lambda value: flip(value, "col", 1)
    core = lambda value: flip(value, "row", 1)

    def core_pieces(value, *ends):
        ends = (*ends, value.shape[0])
        return [core(value[first:end]) for first, end in zip((0, *ends), ends)]

    own, other = part(dev, "part_orbitals", filtered)
    near = across(other)
    image, image_other = part(dev, "part_images", hamiltonian_applied)
    image_near = across(image_other)
    for_core, for_near = part_cores(dev, own, other, image)
    far = across(for_near)
    own_core, from_core = core(own), core(for_core)
    rotated = rotate(dev, filtered, rotation)

    def reduced_x(rows, keep, send):
        total = Sum(rows, (keep,), (dev.swap(send, dev.x_top),))
        for bit in dev.x_rest:
            halve(dev, [total], "x", bit)
        return total

    near_core = core_pieces(after(near, rotated), cells // 2)
    columns = [own, own_core, near, *near_core]
    this = lambda xi, at: (0, 2 * xi + at[0])
    rows = Rows(dev, *((array, array.shape[0], this) for array in columns))
    same = reduced_x(half + lower_rows(dev), *overlap(dev, rows, columns, True))

    images = [image, from_core, image_near, *core_pieces(after(image_near, dev.last), cells * 3 // 8, cells * 11 // 16)]
    even = reduced_x(b, *project(dev, rows, 0, b, images, (0, 2)))
    halve(dev, [same], "z", dev.z_bits[0])
    odd = reduced_x(b, *project(dev, rows, 0, b, images, (1, 2)))
    proj_own = Sum(b)
    proj_own.terms = [(e[0] + o[0], *e[1:]) for e, o in zip(even.terms, odd.terms)]

    far_there = after(far, dev.last)[cells:]
    far_core = core_pieces(far_there, cells // 2)
    dev.wait(even)
    far_rows = Rows(
        dev,
        (other, cells, this),
        (from_core, cells, lambda xi, at: (0, Z + xi)),
        (far, cells, lambda xi, at: (0, xi)),
        *((array, array.shape[0], lambda xi, at: (0, xi)) for array in far_core),
    )
    mixed = reduced_x(half, *overlap(dev, far_rows, columns, False))
    halve(dev, [same], "z", dev.z_bits[1])
    halve(dev, [proj_own], "z", dev.z_bits[0])
    proj_other = [reduced_x(w, *project(dev, far_rows, 0, w, images))]
    for bit in dev.z_bits[2:]:
        halve(dev, [same], "z", bit)
    same = finish(dev, same, scale)
    same_pairs = [
        (i * C + 2 * j + p, j * C + 2 * i + p)
        for i in range(R) for j in range(Z) for p in range(2) if i != j
    ]
    same_half = lax.ppermute(same[:half], ("row", "col"), same_pairs)
    for n in range(1, cuts):
        proj_other.append(reduced_x(w, *project(dev, far_rows, n, w, images)))
    halve(dev, [mixed], "z", dev.z_bits[0])
    for bit in dev.z_bits[1:]:
        halve(dev, [proj_own], "z", bit)
    for bit in dev.z_bits[1:]:
        halve(dev, [mixed], "z", bit)
    halve(dev, [proj_other[0]], "z", dev.z_bits[0])
    dev.waits.append(same_half)
    for total in proj_other[1:]:
        halve(dev, [total], "z", dev.z_bits[0])
    dev.wait(proj_own)
    for bit in dev.z_bits[1:]:
        halve(dev, [proj_other[0]], "z", bit)
    mixed = finish(dev, mixed, scale)
    mixed_pairs = [
        (i * C + 2 * j + p, j * C + 2 * i + 1 - p)
        for i in range(R) for j in range(Z) for p in range(2)
    ]
    mixed_half = lax.ppermute(mixed, ("row", "col"), mixed_pairs)
    for total in proj_other[1:]:
        for bit in dev.z_bits[1:]:
            halve(dev, [total], "z", bit)
    intersection = assemble_overlap(dev, same, same_half, mixed, mixed_half)

    def assemble(at, values, inputs, outs):
        first = pl.multiple_of(at[1] * b, b)
        second = pl.multiple_of((1 - at[1]) * b, b)
        outs[0][pl.ds(first, b)] = added(values[0], (0, 0)) * scale
        for n in range(cuts):
            outs[0][pl.ds(second + n * w, w)] = added(values[1 + n], (0, 0)) * scale

    (projected,) = gather(
        dev, assemble, "assemble", [proj_own, *proj_other], None, [], [(2 * b, b)]
    )
    return (intersection, projected, rotated)


def solution(mesh):
    return jax.shard_map(
        local,
        mesh=mesh,
        in_specs=(P(("row", "col"), None), P(("row", "col"), None), P()),
        out_specs=(P("row", "col"), P("row", "col"), P(("row", "col"), None)),
        check_vma=False,
    )
```

```python
import jax
import jax.numpy as jnp
from jax import lax
from jax.experimental import pallas as pl
from jax.experimental.pallas import tpu as pltpu
from jax.sharding import PartitionSpec as P


VMEM_LIMIT = 48 * 2**20


def split(value):
    high = value.astype(jnp.bfloat16)
    return high, (value - high.astype(jnp.float32)).astype(jnp.bfloat16)


def multiply(left, right):
    dot = lambda a, b: jnp.dot(a, b, preferred_element_type=jnp.float32)
    (lh, ll), (rh, rl) = left, right
    return dot(lh, rh) + (dot(ll, rh) + dot(lh, rl))


def multiply_stacked(left, right):
    rows = left.shape[0] // 2
    both = jnp.dot(left[...], right[0], preferred_element_type=jnp.float32)
    rest = jnp.dot(left[:rows], right[1], preferred_element_type=jnp.float32)
    return both[:rows] + (both[rows:] + rest)


class Device:
    def __init__(self, orbitals):
        self.R, self.C = lax.axis_size("row"), lax.axis_size("col")
        self.X, self.Z = self.R // 2, self.C // 2
        self.b = orbitals // self.C
        r, c = lax.axis_index("row"), lax.axis_index("col")
        self.r, self.c, self.y, self.z = r, c, c % 2, c // 2
        x_bits = self.X.bit_length() - 1
        z_bits = self.Z.bit_length() - 1
        self.bits = [r % 2, self.y]
        self.bits += [(r >> (1 + i)) & 1 for i in range(x_bits)]
        self.bits += [(self.z >> i) & 1 for i in range(z_bits)]
        self.x_top = 1 + x_bits
        self.x_rest = list(range(2, 1 + x_bits))
        self.z_bits = list(range(2 + x_bits, 2 + x_bits + z_bits))
        self.at = jnp.stack(self.bits + [r, self.z]).astype(jnp.int32)
        self.last, self.waits = None, []

    def axis_bit(self, bit):
        if bit < self.z_bits[0]:
            return "row", bit - 1
        return "col", bit - self.z_bits[0] + 1

    def swap(self, value, bit):
        axis, shift = self.axis_bit(bit)
        return flip(value, axis, 1 << shift)

    def wait(self, total):
        self.waits += total.terms[-1][0]

    def call(self, body, name, arrays, in_specs, out_shapes, out_specs, grid=(), scratch=()):
        after = ([] if self.last is None else [self.last]) + self.waits
        self.waits = []
        count = len(arrays)

        def ordered(at, *refs):
            body(at, *refs[:count], *refs[count + len(after) :])

        outs = pl.pallas_call(
            ordered,
            name=name,
            out_shape=[jax.ShapeDtypeStruct(s, jnp.float32) for s in out_shapes],
            grid_spec=pltpu.PrefetchScalarGridSpec(
                num_scalar_prefetch=1,
                grid=grid,
                in_specs=list(in_specs) + [pl.BlockSpec(memory_space=pl.ANY)] * len(after),
                out_specs=list(out_specs),
                scratch_shapes=list(scratch),
            ),
            compiler_params=pltpu.CompilerParams(vmem_limit_bytes=VMEM_LIMIT),
            cost_estimate=pl.CostEstimate(flops=0, bytes_accessed=0, transcendentals=0),
        )(self.at, *arrays, *after)
        self.last = outs[0]
        return outs


def flip(value, axis, mask):
    count = lax.axis_size(axis)
    return lax.ppermute(value, axis, [(i, i ^ mask) for i in range(count)])


VMEM = pl.BlockSpec(memory_space=pltpu.VMEM)


def after(value, other):
    return lax.optimization_barrier((value, other))[0]


def whole(array):
    return pl.BlockSpec(array.shape, lambda i, at: (0,) * array.ndim)


def part(dev, name, array):
    cells, b = array.shape[0], dev.b

    def body(at, source, own, other):
        even, odd = source[:, :b], source[:, b:]
        first = at[1] == 0
        own[...] = jnp.where(first, even, odd)
        other[...] = jnp.where(first, odd, even)

    block = lambda width: pl.BlockSpec((cells, width), lambda i, at: (0, i))
    return dev.call(
        body, name, [array], [block(2 * b)], [(cells, dev.R * b)] * 2,
        [block(b)] * 2, grid=(dev.R,),
    )


def part_cores(dev, own, other, image):
    cells, b, X, Z = own.shape[0], dev.b, dev.X, dev.Z
    n = Z * b

    def body(at, image, other, own, for_core, for_near):
        for_core[:, :n] = image[...]
        for xi in range(X):
            block = slice(xi * b, (xi + 1) * b)
            for side in range(2):
                r = slice((2 * xi + side) * b, (2 * xi + side + 1) * b)

                @pl.when(at[0] == side)
                def _(block=block, r=r):
                    for_near[:cells, block] = own[:, r]

                @pl.when(at[0] != side)
                def _(block=block, r=r, xi=xi):
                    for_near[cells:, block] = own[:, r]
                    for_core[:, n + xi * b : n + (xi + 1) * b] = other[:, r]

    return dev.call(
        body, "part_cores", [image, other, own], [VMEM] * 3,
        [(cells, n + X * b), (2 * cells, X * b)], [VMEM] * 2,
    )


class Rows:
    def __init__(self, dev, *sources):
        self.X = dev.X
        self.arrays, self.specs, self.cells = [], [], []
        for array, cells, index in sources:
            self.cells.append(cells)
            for xi in range(dev.X):
                self.arrays.append(array)
                self.specs.append(
                    pl.BlockSpec((cells, dev.b), lambda i, at, xi=xi, index=index: index(xi, at))
                )

    def blocks(self, refs):
        return [
            [ref[...] for ref in refs[m * self.X : (m + 1) * self.X]]
            for m in range(len(self.cells))
        ]


def column_blocks(dev, name, rows, cut, width, columns, zs, writes, out_rows):
    X, b = dev.X, dev.b
    top = X // 2
    first, stride = zs
    steps = dev.Z // stride
    nr, nc = len(rows.arrays), len(columns)
    total = sum(rows.cells)

    def body(at, *refs):
        lefts, rights = refs[:nr], refs[nr : nr + nc]
        keep, send, left = refs[nr + nc :]

        @pl.when(pl.program_id(0) == 0)
        def _():
            start = 0
            for cells, blocks in zip(rows.cells, rows.blocks(lefts)):
                for xi, block in enumerate(blocks):
                    at_cells = slice(start, start + cells)
                    first = slice(xi * width, (xi + 1) * width)
                    second = slice((X + xi) * width, (X + xi + 1) * width)
                    turned = block.T[cut * width : (cut + 1) * width]
                    left[first, at_cells], left[second, at_cells] = split(turned)
                start += cells

        right = split(jnp.concatenate([ref[...] for ref in rights], 0))
        value = multiply_stacked(left, right)
        zz = stride * pl.program_id(0) + first
        for xi in range(X):
            part = value[xi * width : (xi + 1) * width]
            for side, target in ((at[dev.x_top], keep), (1 - at[dev.x_top], send)):
                for at_rows, condition, result in writes(at, 2 * xi + at[0], zz, part):
                    flag = side == xi // top
                    if condition is not None:
                        flag = jnp.logical_and(flag, condition)

                    @pl.when(flag)
                    def _(target=target, at_rows=at_rows, result=result):
                        target[xi % top, 0, at_rows] = result()

    out = pl.BlockSpec((top, 1, out_rows, b), lambda i, at: (0, i, 0, 0))
    return dev.call(
        body, name, [*rows.arrays, *columns],
        rows.specs
        + [
            pl.BlockSpec((array.shape[0], b), lambda i, at: (0, stride * i + first))
            for array in columns
        ],
        [(top, steps, out_rows, b)] * 2, [out] * 2, grid=(steps,),
        scratch=[pltpu.VMEM((2 * X * width, total), jnp.bfloat16)],
    )


def project(dev, rows, cut, width, images, zs=(0, 1)):
    writes = lambda at, r, zz, part: [(slice(None), None, lambda: part)]
    return column_blocks(dev, "project", rows, cut, width, images, zs, writes, width)


def lower_rows(dev):
    half = dev.b // 2
    return half // 2 if half % 128 == 0 else half


def overlap(dev, rows, columns, same):
    b = dev.b
    half = b // 2
    more = lower_rows(dev) if same else 0

    def mirrored(part):
        return part[:, half:].T if half % 128 == 0 else part.T[half:]

    def lower(part):
        if more == half:
            return part[half:]
        corner = part[half:, half:]
        return jnp.concatenate([corner[:more], corner[more:]], 1)

    def writes(at, r, zz, part):
        straight = (r <= zz) if same else (at[1] == 0)
        out = [
            (slice(0, half), straight, lambda: part[:half]),
            (slice(0, half), jnp.logical_not(straight), lambda: mirrored(part)),
        ]
        if same:
            out += [
                (slice(half, half + more), r == zz, lambda: lower(part)),
                (slice(half, half + more), r != zz, lambda: jnp.zeros((more, b), jnp.float32)),
            ]
        return out

    return column_blocks(
        dev, "overlap_same" if same else "overlap_mixed", rows, 0, b, columns, (0, 1),
        writes, half + more,
    )


class Sum:
    def __init__(self, rows, *terms):
        self.rows = rows
        self.terms = [(term, [], [], 0) for term in terms]

    def counts(self):
        arrays, xs, zs, _ = self.terms[0]
        n0, n1 = arrays[0].shape[:2]
        return n0 >> len(xs), (n1 * len(arrays)) >> len(zs)


def gather(dev, body, name, sums, pick, arrays_in, out_shapes):
    arrays, slots, shapes = [], [], []
    for total in sums:
        n0, n1 = total.counts()
        if pick == "every":
            n1 = dev.Z - 1
        elif pick is not None:
            n0, n1 = (n0 // 2, n1) if pick[0] == "x" else (n0, n1 // 2)
        for term, _, _, _ in total.terms:
            slots.append(list(range(len(arrays), len(arrays) + len(term))))
            arrays += term
            shapes.append((n0, n1, total.rows, dev.b))
    count, more = len(arrays), len(arrays_in)

    def kernel(at, *refs):
        sources, refs = refs[:count], refs[count:]
        inputs, refs = refs[:more], refs[more:]
        outs, refs = refs[: len(out_shapes)], refs[len(out_shapes) :]
        buffers, sems = refs[:-1], refs[-1]
        waits, k = [], 0
        for total in sums:
            for _, xs, zs, row in total.terms:
                n0, n1, rows, _ = shapes[k]
                xs = [at[bit] for bit in xs]
                zs = [at[bit] for bit in zs]
                if pick == "every":
                    zs = []
                elif pick is not None:
                    (xs if pick[0] == "x" else zs).append(1 - at[pick[1]])
                x_step, z_step = 1 << len(xs), 1 << len(zs)
                x_base = sum((v << i for i, v in enumerate(xs)), 0)
                z_base = sum((v << i for i, v in enumerate(zs)), 0)
                for i in range(n0):
                    for j in range(n1):
                        xi, zi = i * x_step + x_base, j * z_step + z_base
                        if pick == "every":
                            zi = at[len(dev.bits) + 1] ^ (j + 1)
                        target, sem = buffers[k].at[i, j], sems.at[k, i * n1 + j]
                        pair = [sources[slot] for slot in slots[k]]
                        take = zi if len(pair) == 1 else zi // 2
                        copies = [
                            pltpu.make_async_copy(ref.at[xi, take, pl.ds(row, rows)], target, sem)
                            for ref in pair
                        ]
                        if len(pair) == 1:
                            copies[0].start()
                        else:
                            for parity in range(2):
                                pl.when(zi % 2 == parity)(copies[parity].start)
                        waits.append(copies[0])
                k += 1
        for copy in waits:
            copy.wait()
        values, k = [], 0
        for total in sums:
            values.append(buffers[k : k + len(total.terms)])
            k += len(total.terms)
        body(at, values, inputs, outs)

    most = max(shape[0] * shape[1] for shape in shapes)
    return dev.call(
        kernel, name, arrays + arrays_in,
        [pl.BlockSpec(memory_space=pl.ANY)] * count + [VMEM] * more,
        out_shapes, [VMEM] * len(out_shapes),
        scratch=[pltpu.VMEM(shape, jnp.float32) for shape in shapes]
        + [pltpu.SemaphoreType.DMA((len(shapes), most))],
    )


def added(buffers, index):
    total = buffers[0][index]
    for buffer in buffers[1:]:
        total = total + buffer[index]
    return total


def halve(dev, sums, kind, bit):
    n0, n1 = sums[0].counts()
    n0, n1 = (n0 // 2, n1) if kind == "x" else (n0, n1 // 2)
    firsts = [sum(total.rows for total in sums[:k]) for k in range(len(sums) + 1)]

    def body(at, values, inputs, outs):
        for k, total in enumerate(sums):
            for i in range(n0):
                for j in range(n1):
                    outs[0][i, j, firsts[k] : firsts[k + 1]] = added(values[k], (i, j))

    (out,) = gather(
        dev, body, "halve", sums, (kind, bit), [], [(n0, n1, firsts[-1], dev.b)]
    )
    came = dev.swap(out, bit)
    for first, total in zip(firsts, sums):
        total.terms = [
            (arrays, xs + [bit] * (kind == "x"), zs + [bit] * (kind == "z"), row)
            for arrays, xs, zs, row in total.terms
        ] + [((came,), [], [], first)]


def scatter(dev, sums):
    firsts = [sum(total.rows for total in sums[:k]) for k in range(len(sums) + 1)]
    n0 = sums[0].counts()[0]
    others = range(1, dev.Z)

    def body(at, values, inputs, outs):
        for j, out in enumerate(outs):
            for k, total in enumerate(sums):
                for i in range(n0):
                    out[i, 0, firsts[k] : firsts[k + 1]] = added(values[k], (i, j))

    outs = gather(
        dev, body, "scatter", sums, "every", [], [(n0, 1, firsts[-1], dev.b) for _ in others]
    )
    came = [flip(out, "col", 2 * mask) for mask, out in zip(others, outs)]
    for first, total in zip(firsts, sums):
        total.terms = [(arrays, xs, dev.z_bits, row) for arrays, xs, zs, row in total.terms]
        total.terms += [((array,), [], [], first) for array in came]


def finish(dev, total, scale):
    def body(at, values, inputs, outs):
        outs[0][...] = added(values[0], (0, 0)) * scale

    return gather(dev, body, "finish", [total], None, [], [(total.rows, dev.b)])[0]


def assemble_overlap(dev, same, same_half, mixed, mixed_half):
    b = dev.b
    half = b // 2
    more = lower_rows(dev)
    last = len(dev.bits)

    def body(at, same, same_half, mixed, mixed_half, out):
        r, z = at[last], at[last + 1]
        first = pl.multiple_of(at[1] * b, b)
        second = pl.multiple_of((1 - at[1]) * b, b)
        mine = same[:half]

        @pl.when(r < z)
        def _():
            out[pl.ds(first, b)] = jnp.concatenate([mine, same_half[...]], 0)

        @pl.when(r > z)
        def _():
            out[pl.ds(first, b)] = jnp.concatenate([same_half[...], mine], 0).T

        @pl.when(r == z)
        def _():
            lower = same[half:]
            if more < half:
                corner = jnp.concatenate([lower[:, :half], lower[:, half:]], 0)
                lower = jnp.concatenate([mine[:, half:].T, corner], 1)
            out[pl.ds(first, b)] = jnp.concatenate([mine, lower], 0)

        @pl.when(at[1] == 0)
        def _():
            out[pl.ds(second, b)] = jnp.concatenate([mixed[...], mixed_half[...]], 0)

        @pl.when(at[1] == 1)
        def _():
            out[pl.ds(second, b)] = jnp.concatenate([mixed_half[...], mixed[...]], 0).T

    arrays = [same, same_half, mixed, mixed_half]
    return dev.call(
        body, "assemble_overlap", arrays, [VMEM] * 4, [(2 * b, b)], [VMEM]
    )[0]


def rotate(dev, array, rotation):
    cells, orbitals = array.shape
    width = 256 if orbitals % 256 == 0 else orbitals

    def body(at, array, block, out, high, low):
        @pl.when(pl.program_id(0) == 0)
        def _():
            high[...], low[...] = split(array[...])

        out[...] = multiply((high[...], low[...]), split(block[...]))

    return dev.call(
        body, "rotate", [array, rotation],
        [whole(array), pl.BlockSpec((orbitals, width), lambda i, at: (0, i))],
        [array.shape], [pl.BlockSpec((cells, width), lambda i, at: (0, i))],
        grid=(orbitals // width,),
        scratch=[pltpu.VMEM((cells, orbitals), jnp.bfloat16)] * 2,
    )[0]


def local(filtered, hamiltonian_applied, rotation):
    cells, orbitals = filtered.shape
    dev = Device(orbitals)
    R, C, Z, b = dev.R, dev.C, dev.Z, dev.b
    half = b // 2
    scale = 1.0 / (cells * C * R)
    cuts = 2 if b % 256 == 0 else 1
    w = b // cuts

    across = lambda value: flip(value, "col", 1)
    core = lambda value: flip(value, "row", 1)

    def core_pieces(value, *ends):
        ends = (*ends, value.shape[0])
        return [core(value[first:end]) for first, end in zip((0, *ends), ends)]

    own, other = part(dev, "part_orbitals", filtered)
    near = across(other)
    image, image_other = part(dev, "part_images", hamiltonian_applied)
    image_near = across(image_other)
    for_core, for_near = part_cores(dev, own, other, image)
    far = across(for_near)
    own_core, from_core = core(own), core(for_core)
    rotated = rotate(dev, filtered, rotation)

    def reduced_x(rows, keep, send):
        total = Sum(rows, (keep,), (dev.swap(send, dev.x_top),))
        for bit in dev.x_rest:
            halve(dev, [total], "x", bit)
        return total

    near_core = core_pieces(after(near, rotated), cells // 2)
    columns = [own, own_core, near, *near_core]
    this = lambda xi, at: (0, 2 * xi + at[0])
    rows = Rows(dev, *((array, array.shape[0], this) for array in columns))
    same = reduced_x(half + lower_rows(dev), *overlap(dev, rows, columns, True))

    images = [image, from_core, image_near, *core_pieces(after(image_near, dev.last), cells * 3 // 8, cells * 11 // 16)]
    even = reduced_x(b, *project(dev, rows, 0, b, images, (0, 2)))
    halve(dev, [same], "z", dev.z_bits[0])
    odd = reduced_x(b, *project(dev, rows, 0, b, images, (1, 2)))
    proj_own = Sum(b)
    proj_own.terms = [(e[0] + o[0], *e[1:]) for e, o in zip(even.terms, odd.terms)]

    far_there = after(far, dev.last)[cells:]
    far_core = core_pieces(far_there, cells // 2)
    dev.wait(even)
    far_rows = Rows(
        dev,
        (other, cells, this),
        (from_core, cells, lambda xi, at: (0, Z + xi)),
        (far, cells, lambda xi, at: (0, xi)),
        *((array, array.shape[0], lambda xi, at: (0, xi)) for array in far_core),
    )
    mixed = reduced_x(half, *overlap(dev, far_rows, columns, False))
    halve(dev, [same], "z", dev.z_bits[1])
    halve(dev, [proj_own], "z", dev.z_bits[0])
    proj_other = [reduced_x(w, *project(dev, far_rows, 0, w, images))]
    for bit in dev.z_bits[2:]:
        halve(dev, [same], "z", bit)
    same = finish(dev, same, scale)
    same_pairs = [
        (i * C + 2 * j + p, j * C + 2 * i + p)
        for i in range(R) for j in range(Z) for p in range(2) if i != j
    ]
    same_half = lax.ppermute(same[:half], ("row", "col"), same_pairs)
    for n in range(1, cuts):
        proj_other.append(reduced_x(w, *project(dev, far_rows, n, w, images)))
    halve(dev, [mixed], "z", dev.z_bits[0])
    for bit in dev.z_bits[1:]:
        halve(dev, [proj_own], "z", bit)
    for bit in dev.z_bits[1:]:
        halve(dev, [mixed], "z", bit)
    halve(dev, [proj_other[0]], "z", dev.z_bits[0])
    dev.waits.append(same_half)
    for total in proj_other[1:]:
        halve(dev, [total], "z", dev.z_bits[0])
    dev.wait(proj_own)
    for bit in dev.z_bits[1:]:
        halve(dev, [proj_other[0]], "z", bit)
    mixed = finish(dev, mixed, scale)
    mixed_pairs = [
        (i * C + 2 * j + p, j * C + 2 * i + 1 - p)
        for i in range(R) for j in range(Z) for p in range(2)
    ]
    mixed_half = lax.ppermute(mixed, ("row", "col"), mixed_pairs)
    for total in proj_other[1:]:
        for bit in dev.z_bits[1:]:
            halve(dev, [total], "z", bit)
    intersection = assemble_overlap(dev, same, same_half, mixed, mixed_half)

    def assemble(at, values, inputs, outs):
        first = pl.multiple_of(at[1] * b, b)
        second = pl.multiple_of((1 - at[1]) * b, b)
        outs[0][pl.ds(first, b)] = added(values[0], (0, 0)) * scale
        for n in range(cuts):
            outs[0][pl.ds(second + n * w, w)] = added(values[1 + n], (0, 0)) * scale

    (projected,) = gather(
        dev, assemble, "assemble", [proj_own, *proj_other], None, [], [(2 * b, b)]
    )
    return (intersection, projected, rotated)


def solution(mesh):
    return jax.shard_map(
        local,
        mesh=mesh,
        in_specs=(P(("row", "col"), None), P(("row", "col"), None), P()),
        out_specs=(P("row", "col"), P("row", "col"), P(("row", "col"), None)),
        check_vma=False,
    )
```

```python
import jax
import jax.numpy as jnp
from jax import lax
from jax.experimental import pallas as pl
from jax.experimental.pallas import tpu as pltpu
from jax.sharding import PartitionSpec as P


VMEM_LIMIT = 48 * 2**20


def split(value):
    high = value.astype(jnp.bfloat16)
    return high, (value - high.astype(jnp.float32)).astype(jnp.bfloat16)


def multiply(left, right):
    dot = lambda a, b: jnp.dot(a, b, preferred_element_type=jnp.float32)
    (lh, ll), (rh, rl) = left, right
    return dot(lh, rh) + (dot(ll, rh) + dot(lh, rl))


class Device:
    def __init__(self, orbitals):
        self.R, self.C = lax.axis_size("row"), lax.axis_size("col")
        self.X, self.Z = self.R // 2, self.C // 2
        self.b = orbitals // self.C
        r, c = lax.axis_index("row"), lax.axis_index("col")
        self.r, self.c, self.y, self.z = r, c, c % 2, c // 2
        x_bits = self.X.bit_length() - 1
        z_bits = self.Z.bit_length() - 1
        self.bits = [r % 2, self.y]
        self.bits += [(r >> (1 + i)) & 1 for i in range(x_bits)]
        self.bits += [(self.z >> i) & 1 for i in range(z_bits)]
        self.x_top = 1 + x_bits
        self.x_rest = list(range(2, 1 + x_bits))
        self.z_bits = list(range(2 + x_bits, 2 + x_bits + z_bits))
        self.at = jnp.stack(self.bits + [r, self.z]).astype(jnp.int32)
        self.last, self.waits = None, []

    def axis_bit(self, bit):
        if bit < self.z_bits[0]:
            return "row", bit - 1
        return "col", bit - self.z_bits[0] + 1

    def swap(self, value, bit):
        axis, shift = self.axis_bit(bit)
        return flip(value, axis, 1 << shift)

    def wait(self, total):
        self.waits += total.terms[-1][0]

    def call(self, body, name, arrays, in_specs, out_shapes, out_specs, grid=(), scratch=()):
        after = ([] if self.last is None else [self.last]) + self.waits
        self.waits = []
        count = len(arrays)

        def ordered(at, *refs):
            body(at, *refs[:count], *refs[count + len(after) :])

        outs = pl.pallas_call(
            ordered,
            name=name,
            out_shape=[jax.ShapeDtypeStruct(s, jnp.float32) for s in out_shapes],
            grid_spec=pltpu.PrefetchScalarGridSpec(
                num_scalar_prefetch=1,
                grid=grid,
                in_specs=list(in_specs) + [pl.BlockSpec(memory_space=pl.ANY)] * len(after),
                out_specs=list(out_specs),
                scratch_shapes=list(scratch),
            ),
            compiler_params=pltpu.CompilerParams(vmem_limit_bytes=VMEM_LIMIT),
            cost_estimate=pl.CostEstimate(flops=0, bytes_accessed=0, transcendentals=0),
        )(self.at, *arrays, *after)
        self.last = outs[0]
        return outs


def flip(value, axis, mask):
    count = lax.axis_size(axis)
    return lax.ppermute(value, axis, [(i, i ^ mask) for i in range(count)])


VMEM = pl.BlockSpec(memory_space=pltpu.VMEM)


def after(value, other):
    return lax.optimization_barrier((value, other))[0]


def whole(array):
    return pl.BlockSpec(array.shape, lambda i, at: (0,) * array.ndim)


def part(dev, name, array):
    cells, b = array.shape[0], dev.b

    def body(at, source, own, other):
        even, odd = source[:, :b], source[:, b:]
        first = at[1] == 0
        own[...] = jnp.where(first, even, odd)
        other[...] = jnp.where(first, odd, even)

    block = lambda width: pl.BlockSpec((cells, width), lambda i, at: (0, i))
    return dev.call(
        body, name, [array], [block(2 * b)], [(cells, dev.R * b)] * 2,
        [block(b)] * 2, grid=(dev.R,),
    )


def part_cores(dev, own, other, image):
    cells, b, X, Z = own.shape[0], dev.b, dev.X, dev.Z
    n = Z * b

    def body(at, image, other, own, for_core, for_near):
        for_core[:, :n] = image[...]
        for xi in range(X):
            block = slice(xi * b, (xi + 1) * b)
            for side in range(2):
                r = slice((2 * xi + side) * b, (2 * xi + side + 1) * b)

                @pl.when(at[0] == side)
                def _(block=block, r=r):
                    for_near[:cells, block] = own[:, r]

                @pl.when(at[0] != side)
                def _(block=block, r=r, xi=xi):
                    for_near[cells:, block] = own[:, r]
                    for_core[:, n + xi * b : n + (xi + 1) * b] = other[:, r]

    return dev.call(
        body, "part_cores", [image, other, own], [VMEM] * 3,
        [(cells, n + X * b), (2 * cells, X * b)], [VMEM] * 2,
    )


class Rows:
    def __init__(self, dev, *sources):
        self.X = dev.X
        self.arrays, self.specs, self.cells = [], [], []
        for array, cells, index in sources:
            self.cells.append(cells)
            for xi in range(dev.X):
                self.arrays.append(array)
                self.specs.append(
                    pl.BlockSpec((cells, dev.b), lambda i, at, xi=xi, index=index: index(xi, at))
                )

    def blocks(self, refs):
        return [
            [ref[...] for ref in refs[m * self.X : (m + 1) * self.X]]
            for m in range(len(self.cells))
        ]


def column_blocks(dev, name, rows, cut, width, columns, zs, writes, out_rows):
    X, b = dev.X, dev.b
    top = X // 2
    first, stride = zs
    steps = dev.Z // stride
    nr, nc = len(rows.arrays), len(columns)
    total = sum(rows.cells)

    def body(at, *refs):
        lefts, rights = refs[:nr], refs[nr : nr + nc]
        keep, send, high, low = refs[nr + nc :]

        @pl.when(pl.program_id(0) == 0)
        def _():
            start = 0
            for cells, blocks in zip(rows.cells, rows.blocks(lefts)):
                for xi, block in enumerate(blocks):
                    index = (slice(xi * width, (xi + 1) * width), slice(start, start + cells))
                    turned = block.T[cut * width : (cut + 1) * width]
                    high[index], low[index] = split(turned)
                start += cells

        right = split(jnp.concatenate([ref[...] for ref in rights], 0))
        value = multiply((high[...], low[...]), right)
        zz = stride * pl.program_id(0) + first
        for xi in range(X):
            part = value[xi * width : (xi + 1) * width]
            for side, target in ((at[dev.x_top], keep), (1 - at[dev.x_top], send)):
                for at_rows, condition, result in writes(at, 2 * xi + at[0], zz, part):
                    flag = side == xi // top
                    if condition is not None:
                        flag = jnp.logical_and(flag, condition)

                    @pl.when(flag)
                    def _(target=target, at_rows=at_rows, result=result):
                        target[xi % top, 0, at_rows] = result()

    out = pl.BlockSpec((top, 1, out_rows, b), lambda i, at: (0, i, 0, 0))
    return dev.call(
        body, name, [*rows.arrays, *columns],
        rows.specs
        + [
            pl.BlockSpec((array.shape[0], b), lambda i, at: (0, stride * i + first))
            for array in columns
        ],
        [(top, steps, out_rows, b)] * 2, [out] * 2, grid=(steps,),
        scratch=[pltpu.VMEM((X * width, total), jnp.bfloat16)] * 2,
    )


def project(dev, rows, cut, width, images, zs=(0, 1)):
    writes = lambda at, r, zz, part: [(slice(None), None, lambda: part)]
    return column_blocks(dev, "project", rows, cut, width, images, zs, writes, width)


def lower_rows(dev):
    half = dev.b // 2
    return half // 2 if half % 128 == 0 else half


def overlap(dev, rows, columns, same):
    b = dev.b
    half = b // 2
    more = lower_rows(dev) if same else 0

    def mirrored(part):
        return part[:, half:].T if half % 128 == 0 else part.T[half:]

    def lower(part):
        if more == half:
            return part[half:]
        corner = part[half:, half:]
        return jnp.concatenate([corner[:more], corner[more:]], 1)

    def writes(at, r, zz, part):
        straight = (r <= zz) if same else (at[1] == 0)
        out = [
            (slice(0, half), straight, lambda: part[:half]),
            (slice(0, half), jnp.logical_not(straight), lambda: mirrored(part)),
        ]
        if same:
            out += [
                (slice(half, half + more), r == zz, lambda: lower(part)),
                (slice(half, half + more), r != zz, lambda: jnp.zeros((more, b), jnp.float32)),
            ]
        return out

    return column_blocks(
        dev, "overlap_same" if same else "overlap_mixed", rows, 0, b, columns, (0, 1),
        writes, half + more,
    )


class Sum:
    def __init__(self, rows, *terms):
        self.rows = rows
        self.terms = [(term, [], [], 0) for term in terms]

    def counts(self):
        arrays, xs, zs, _ = self.terms[0]
        n0, n1 = arrays[0].shape[:2]
        return n0 >> len(xs), (n1 * len(arrays)) >> len(zs)


class Arriving:
    def __init__(self, values, waits):
        self.values, self.waits = values, waits

    def __getitem__(self, k):
        for copy in self.waits[k]:
            copy.wait()
        self.waits[k] = []
        return self.values[k]


def gather(dev, body, name, sums, pick, arrays_in, out_shapes):
    arrays, slots, shapes = [], [], []
    for total in sums:
        n0, n1 = total.counts()
        if pick == "every":
            n1 = dev.Z - 1
        elif pick is not None:
            n0, n1 = (n0 // 2, n1) if pick[0] == "x" else (n0, n1 // 2)
        for term, _, _, _ in total.terms:
            slots.append(list(range(len(arrays), len(arrays) + len(term))))
            arrays += term
            shapes.append((n0, n1, total.rows, dev.b))
    count, more = len(arrays), len(arrays_in)

    def kernel(at, *refs):
        sources, refs = refs[:count], refs[count:]
        inputs, refs = refs[:more], refs[more:]
        outs, refs = refs[: len(out_shapes)], refs[len(out_shapes) :]
        buffers, sems = refs[:-1], refs[-1]
        waits, k = [], 0
        for total in sums:
            waits.append([])
            for _, xs, zs, row in total.terms:
                n0, n1, rows, _ = shapes[k]
                xs = [at[bit] for bit in xs]
                zs = [at[bit] for bit in zs]
                if pick == "every":
                    zs = []
                elif pick is not None:
                    (xs if pick[0] == "x" else zs).append(1 - at[pick[1]])
                x_step, z_step = 1 << len(xs), 1 << len(zs)
                x_base = sum((v << i for i, v in enumerate(xs)), 0)
                z_base = sum((v << i for i, v in enumerate(zs)), 0)
                for i in range(n0):
                    for j in range(n1):
                        xi, zi = i * x_step + x_base, j * z_step + z_base
                        if pick == "every":
                            zi = at[len(dev.bits) + 1] ^ (j + 1)
                        target, sem = buffers[k].at[i, j], sems.at[k, i * n1 + j]
                        pair = [sources[slot] for slot in slots[k]]
                        take = zi if len(pair) == 1 else zi // 2
                        copies = [
                            pltpu.make_async_copy(ref.at[xi, take, pl.ds(row, rows)], target, sem)
                            for ref in pair
                        ]
                        if len(pair) == 1:
                            copies[0].start()
                        else:
                            for parity in range(2):
                                pl.when(zi % 2 == parity)(copies[parity].start)
                        waits[-1].append(copies[0])
                k += 1
        values, k = [], 0
        for total in sums:
            values.append(buffers[k : k + len(total.terms)])
            k += len(total.terms)
        body(at, Arriving(values, waits), inputs, outs)

    most = max(shape[0] * shape[1] for shape in shapes)
    return dev.call(
        kernel, name, arrays + arrays_in,
        [pl.BlockSpec(memory_space=pl.ANY)] * count + [VMEM] * more,
        out_shapes, [VMEM] * len(out_shapes),
        scratch=[pltpu.VMEM(shape, jnp.float32) for shape in shapes]
        + [pltpu.SemaphoreType.DMA((len(shapes), most))],
    )


def added(buffers, index):
    total = buffers[0][index]
    for buffer in buffers[1:]:
        total = total + buffer[index]
    return total


def halve(dev, sums, kind, bit):
    n0, n1 = sums[0].counts()
    n0, n1 = (n0 // 2, n1) if kind == "x" else (n0, n1 // 2)
    firsts = [sum(total.rows for total in sums[:k]) for k in range(len(sums) + 1)]

    def body(at, values, inputs, outs):
        for k, total in enumerate(sums):
            for i in range(n0):
                for j in range(n1):
                    outs[0][i, j, firsts[k] : firsts[k + 1]] = added(values[k], (i, j))

    (out,) = gather(
        dev, body, "halve", sums, (kind, bit), [], [(n0, n1, firsts[-1], dev.b)]
    )
    came = dev.swap(out, bit)
    for first, total in zip(firsts, sums):
        total.terms = [
            (arrays, xs + [bit] * (kind == "x"), zs + [bit] * (kind == "z"), row)
            for arrays, xs, zs, row in total.terms
        ] + [((came,), [], [], first)]


def scatter(dev, sums):
    firsts = [sum(total.rows for total in sums[:k]) for k in range(len(sums) + 1)]
    n0 = sums[0].counts()[0]
    others = range(1, dev.Z)

    def body(at, values, inputs, outs):
        for j, out in enumerate(outs):
            for k, total in enumerate(sums):
                for i in range(n0):
                    out[i, 0, firsts[k] : firsts[k + 1]] = added(values[k], (i, j))

    outs = gather(
        dev, body, "scatter", sums, "every", [], [(n0, 1, firsts[-1], dev.b) for _ in others]
    )
    came = [flip(out, "col", 2 * mask) for mask, out in zip(others, outs)]
    for first, total in zip(firsts, sums):
        total.terms = [(arrays, xs, dev.z_bits, row) for arrays, xs, zs, row in total.terms]
        total.terms += [((array,), [], [], first) for array in came]


def finish(dev, total, scale):
    def body(at, values, inputs, outs):
        outs[0][...] = added(values[0], (0, 0)) * scale

    return gather(dev, body, "finish", [total], None, [], [(total.rows, dev.b)])[0]


def assemble_overlap(dev, same, same_half, mixed, mixed_half):
    b = dev.b
    half = b // 2
    more = lower_rows(dev)
    last = len(dev.bits)

    def body(at, same, same_half, mixed, mixed_half, out):
        r, z = at[last], at[last + 1]
        first = pl.multiple_of(at[1] * b, b)
        second = pl.multiple_of((1 - at[1]) * b, b)
        mine = same[:half]

        @pl.when(r < z)
        def _():
            out[pl.ds(first, b)] = jnp.concatenate([mine, same_half[...]], 0)

        @pl.when(r > z)
        def _():
            out[pl.ds(first, b)] = jnp.concatenate([same_half[...], mine], 0).T

        @pl.when(r == z)
        def _():
            lower = same[half:]
            if more < half:
                corner = jnp.concatenate([lower[:, :half], lower[:, half:]], 0)
                lower = jnp.concatenate([mine[:, half:].T, corner], 1)
            out[pl.ds(first, b)] = jnp.concatenate([mine, lower], 0)

        @pl.when(at[1] == 0)
        def _():
            out[pl.ds(second, b)] = jnp.concatenate([mixed[...], mixed_half[...]], 0)

        @pl.when(at[1] == 1)
        def _():
            out[pl.ds(second, b)] = jnp.concatenate([mixed_half[...], mixed[...]], 0).T

    arrays = [same, same_half, mixed, mixed_half]
    return dev.call(
        body, "assemble_overlap", arrays, [VMEM] * 4, [(2 * b, b)], [VMEM]
    )[0]


def rotate(dev, array, rotation):
    cells, orbitals = array.shape
    width = 256 if orbitals % 256 == 0 else orbitals

    def body(at, array, block, out, high, low):
        @pl.when(pl.program_id(0) == 0)
        def _():
            high[...], low[...] = split(array[...])

        out[...] = multiply((high[...], low[...]), split(block[...]))

    return dev.call(
        body, "rotate", [array, rotation],
        [whole(array), pl.BlockSpec((orbitals, width), lambda i, at: (0, i))],
        [array.shape], [pl.BlockSpec((cells, width), lambda i, at: (0, i))],
        grid=(orbitals // width,),
        scratch=[pltpu.VMEM((cells, orbitals), jnp.bfloat16)] * 2,
    )[0]


def local(filtered, hamiltonian_applied, rotation):
    cells, orbitals = filtered.shape
    dev = Device(orbitals)
    R, C, Z, b = dev.R, dev.C, dev.Z, dev.b
    half = b // 2
    scale = 1.0 / (cells * C * R)
    cuts = 2 if b % 256 == 0 else 1
    w = b // cuts

    across = lambda value: flip(value, "col", 1)
    core = lambda value: flip(value, "row", 1)

    def core_pieces(value, *ends):
        ends = (*ends, value.shape[0])
        return [core(value[first:end]) for first, end in zip((0, *ends), ends)]

    own, other = part(dev, "part_orbitals", filtered)
    near = across(other)
    image, image_other = part(dev, "part_images", hamiltonian_applied)
    image_near = across(image_other)
    for_core, for_near = part_cores(dev, own, other, image)
    far = across(for_near)
    own_core, from_core = core(own), core(for_core)
    rotated = rotate(dev, filtered, rotation)

    def reduced_x(rows, keep, send):
        total = Sum(rows, (keep,), (dev.swap(send, dev.x_top),))
        for bit in dev.x_rest:
            halve(dev, [total], "x", bit)
        return total

    near_core = core_pieces(after(near, rotated), cells // 2)
    columns = [own, own_core, near, *near_core]
    this = lambda xi, at: (0, 2 * xi + at[0])
    rows = Rows(dev, *((array, array.shape[0], this) for array in columns))
    same = reduced_x(half + lower_rows(dev), *overlap(dev, rows, columns, True))

    images = [image, from_core, image_near, *core_pieces(after(image_near, dev.last), cells * 3 // 8, cells * 11 // 16)]
    even = reduced_x(b, *project(dev, rows, 0, b, images, (0, 2)))
    halve(dev, [same], "z", dev.z_bits[0])
    odd = reduced_x(b, *project(dev, rows, 0, b, images, (1, 2)))
    proj_own = Sum(b)
    proj_own.terms = [(e[0] + o[0], *e[1:]) for e, o in zip(even.terms, odd.terms)]

    far_there = after(far, dev.last)[cells:]
    far_core = core_pieces(far_there, cells // 2)
    dev.wait(even)
    far_rows = Rows(
        dev,
        (other, cells, this),
        (from_core, cells, lambda xi, at: (0, Z + xi)),
        (far, cells, lambda xi, at: (0, xi)),
        *((array, array.shape[0], lambda xi, at: (0, xi)) for array in far_core),
    )
    mixed = reduced_x(half, *overlap(dev, far_rows, columns, False))
    halve(dev, [same], "z", dev.z_bits[1])
    halve(dev, [proj_own], "z", dev.z_bits[0])
    proj_other = [reduced_x(w, *project(dev, far_rows, 0, w, images))]
    for bit in dev.z_bits[2:]:
        halve(dev, [same], "z", bit)
    same = finish(dev, same, scale)
    same_pairs = [
        (i * C + 2 * j + p, j * C + 2 * i + p)
        for i in range(R) for j in range(Z) for p in range(2) if i != j
    ]
    same_half = lax.ppermute(same[:half], ("row", "col"), same_pairs)
    for n in range(1, cuts):
        proj_other.append(reduced_x(w, *project(dev, far_rows, n, w, images)))
    halve(dev, [mixed], "z", dev.z_bits[0])
    for bit in dev.z_bits[1:]:
        halve(dev, [proj_own], "z", bit)
    for bit in dev.z_bits[1:]:
        halve(dev, [mixed], "z", bit)
    halve(dev, [proj_other[0]], "z", dev.z_bits[0])
    dev.waits.append(same_half)
    for total in proj_other[1:]:
        halve(dev, [total], "z", dev.z_bits[0])
    dev.wait(proj_own)
    for bit in dev.z_bits[1:]:
        halve(dev, [proj_other[0]], "z", bit)
    mixed = finish(dev, mixed, scale)
    mixed_pairs = [
        (i * C + 2 * j + p, j * C + 2 * i + 1 - p)
        for i in range(R) for j in range(Z) for p in range(2)
    ]
    mixed_half = lax.ppermute(mixed, ("row", "col"), mixed_pairs)
    for total in proj_other[1:]:
        for bit in dev.z_bits[1:]:
            halve(dev, [total], "z", bit)
    intersection = assemble_overlap(dev, same, same_half, mixed, mixed_half)

    def assemble(at, values, inputs, outs):
        first = pl.multiple_of(at[1] * b, b)
        second = pl.multiple_of((1 - at[1]) * b, b)
        outs[0][pl.ds(first, b)] = added(values[0], (0, 0)) * scale
        for n in range(cuts):
            outs[0][pl.ds(second + n * w, w)] = added(values[1 + n], (0, 0)) * scale

    (projected,) = gather(
        dev, assemble, "assemble", [proj_own, *proj_other], None, [], [(2 * b, b)]
    )
    return (intersection, projected, rotated)


def solution(mesh):
    return jax.shard_map(
        local,
        mesh=mesh,
        in_specs=(P(("row", "col"), None), P(("row", "col"), None), P()),
        out_specs=(P("row", "col"), P("row", "col"), P(("row", "col"), None)),
        check_vma=False,
    )
```
